512 devices in a mesh: inst: 128 (over x, z, core), tp: 4 (over y).
Axes of the slice: x: 4, y: 4, z: 16, core: 2. Of those that a mesh axis runs over, the one named last changes fastest.
Arguments:
- query: bfloat16 [4, 256, 8192], P(None, 'inst', 'tp'), may hold values from -4.5 to 4.5
- fresh_key_value: bfloat16 [4, 256, 1024], P(None, 'inst', 'tp'), may hold values from -4.5 to 4.5
- kv_pool: bfloat16 [512, 2048, 1024], P('inst', None, 'tp'), may hold values from -4.5 to 4.5
- lengths: int32 [256], P('inst'), may hold values from 1 to 6144, as said below
- slot_owner: int32 [512], P(('inst', 'tp')), may hold values from 0 to 255, as said below
- slot_block: int32 [512], P(('inst', 'tp')), may hold values from 0 to 2, as said below
Outputs:
- attended: bfloat16 [4, 256, 8192], P(None, 'inst', 'tp')
The draws below stay inside these ranges and needn't reach their ends.
Inputs may be any that keep to these rules, and one draw needn't show every extreme that they name: `slot_owner`: every instance owns exactly 4 blocks in the pools (request id // 2 is the owning instance), every request at least one; the 4 slots of one instance's pool belong to 4 different owning instances. `slot_block`: A request's blocks are numbered 0, 1, ... without gaps. `lengths`: A request with n blocks has between (n - 1) * 2048 + 1 and n * 2048 cached tokens.
All inputs are finite; a program needn't handle non-finite values.
Results may differ from the reference program's by a relative error of at most 0.0056.
Values may be sent and summed in bfloat16 or wider, within the bound.
A program may use at most 64 MiB of HBM per device.

```python
import math
import jax
import jax.numpy as jnp
from jax import lax

HEADS_Q = 64
KV_HEADS = 4
HEAD_DIM = 128
BLOCK = 2048
STEPS = 4
REQ_DEV = 2
SLOTS = 4
INSTANCES = 128
REQUESTS = 256


def lending(key):
    keys = jax.random.split(key, 5)
    order = jax.random.permutation(keys[0], INSTANCES)
    offsets = jax.random.permutation(keys[1], INSTANCES)[:SLOTS]
    position = jnp.arange(INSTANCES)
    owners_at = order[(position[:, None] + offsets[None, :]) % INSTANCES]
    owner_inst = jnp.zeros((INSTANCES, SLOTS), jnp.int32).at[order].set(owners_at)
    columns = jnp.arange(SLOTS)
    extra = jax.random.randint(keys[2], (INSTANCES, SLOTS), 0, REQ_DEV)
    base = jnp.where(columns[None, :] < REQ_DEV, columns[None, :], extra)
    base = base.at[0].set(jnp.where(columns < REQ_DEV, columns, 0))
    shuffle = jax.vmap(lambda k: jax.random.permutation(k, SLOTS))(jax.random.split(keys[3], INSTANCES))
    req_of = jnp.take_along_axis(base, shuffle, 1)
    same = req_of[:, :, None] == req_of[:, None, :]
    earlier = columns[None, :] < columns[:, None]
    block_idx = jnp.sum(same & earlier[None], 2).astype(jnp.int32)
    counts = jnp.sum(req_of[:, None, :] == jnp.arange(REQ_DEV)[None, :, None], 2).reshape(-1).astype(jnp.int32)
    request = owner_inst * REQ_DEV + req_of[owner_inst, columns[None, :]]
    block = block_idx[owner_inst, columns[None, :]]
    fill = jax.random.randint(keys[4], (REQUESTS,), 1, BLOCK + 1)
    lengths = (counts - 1) * BLOCK + fill
    lengths = lengths.at[0].set(counts[0] * BLOCK)
    return (request.reshape(-1).astype(jnp.int32), block.reshape(-1).astype(jnp.int32), lengths.astype(jnp.int32))


def draw_slot_owner(key, part):
    return lending(key)[0]


def draw_slot_block(key, part):
    return lending(key)[1]


def draw_lengths(key, part):
    return lending(key)[2]


def draw_query(key, part):
    key = jax.random.fold_in(key, 1)
    shape = (STEPS, REQUESTS, HEADS_Q, HEAD_DIM)
    values = jnp.clip(jax.random.normal(key, shape, jnp.float32), -4.5, 4.5)
    return values.reshape(STEPS, REQUESTS, HEADS_Q * HEAD_DIM).astype(jnp.bfloat16)


def draw_fresh_key_value(key, part):
    key = jax.random.fold_in(key, 2)
    shape = (STEPS, REQUESTS, KV_HEADS, 2, HEAD_DIM)
    values = jnp.clip(jax.random.normal(key, shape, jnp.float32), -4.5, 4.5)
    return values.reshape(STEPS, REQUESTS, KV_HEADS * 2 * HEAD_DIM).astype(jnp.bfloat16)


def draw_kv_pool(key, part):
    key = jax.random.fold_in(key, 3)
    shape = (INSTANCES * SLOTS, BLOCK, KV_HEADS, 2, HEAD_DIM)
    values = jnp.clip(jax.random.normal(key, shape, jnp.float32), -4.5, 4.5)
    return values.reshape(INSTANCES * SLOTS, BLOCK, KV_HEADS * 2 * HEAD_DIM).astype(jnp.bfloat16)


def setup_inputs(seed: int = 0) -> dict:
    splits = jax.random.split(jax.random.key(seed), 7)
    query = draw_query(jax.random.fold_in(splits[6], 71), 0)
    fresh_key_value = draw_fresh_key_value(jax.random.fold_in(splits[6], 71), 0)
    kv_pool = draw_kv_pool(jax.random.fold_in(splits[6], 71), 0)
    lengths = draw_lengths(jax.random.fold_in(splits[6], 71), 0)
    slot_owner = draw_slot_owner(jax.random.fold_in(splits[6], 71), 0)
    slot_block = draw_slot_block(jax.random.fold_in(splits[6], 71), 0)
    return dict(query=query, fresh_key_value=fresh_key_value, kv_pool=kv_pool, lengths=lengths, slot_owner=slot_owner, slot_block=slot_block)


def partial_softmax(scores, valid, values_f32, form):
    top = lax.optimization_barrier(jnp.max(jnp.where(valid, scores, -jnp.inf), -1))
    weights = jnp.where(valid, jnp.exp(scores - top[..., None]), 0.0)
    total = lax.optimization_barrier(jnp.sum(weights, -1))
    rounded = weights.astype(jnp.bfloat16).astype(jnp.float32)
    part = jnp.einsum(form, rounded, values_f32) / total[..., None]
    return (part, top + jnp.log(total))

def reference(query, fresh_key_value, kv_pool, lengths, slot_owner, slot_block):
    group = HEADS_Q // KV_HEADS
    scale = 1.0 / math.sqrt(HEAD_DIM)
    heads = query.reshape(STEPS, REQUESTS, KV_HEADS, group, HEAD_DIM).astype(jnp.float32)

    def one_slot(packed):
        block, owner, index = packed
        q_rows = lax.dynamic_index_in_dim(heads, owner, 1, keepdims=False)
        pairs = block.reshape(BLOCK, KV_HEADS, 2, HEAD_DIM).astype(jnp.float32)
        scores = jnp.einsum('akgd,tkd->kagt', q_rows, pairs[:, :, 0]) * scale
        length = lax.dynamic_index_in_dim(lengths, owner, 0, keepdims=False)
        valid = index * BLOCK + jnp.arange(BLOCK, dtype=jnp.int32) < length
        part, lse = partial_softmax(scores, valid, pairs[:, :, 1], 'kagt,tkd->kagd')
        part = lax.optimization_barrier(part.astype(jnp.bfloat16)).astype(jnp.float32)
        return (part, lse)
    parts, part_lse = lax.map(one_slot, (kv_pool, slot_owner, slot_block))
    fresh = fresh_key_value.reshape(STEPS, REQUESTS, KV_HEADS, 2, HEAD_DIM).astype(jnp.float32)
    tail_score_rows = jnp.einsum('arkgd,brkd->rkagb', heads, fresh[:, :, :, 0]) * scale
    steps_idx = jnp.arange(STEPS, dtype=jnp.int32)
    causal_mask = (steps_idx[:, None] >= steps_idx[None, :])[None, None, :, None, :]
    tail_part, tail_lse = partial_softmax(tail_score_rows, causal_mask, fresh[:, :, :, 1], 'rkagb,brkd->rkagd')
    peak = jnp.full(tail_lse.shape, -jnp.inf, dtype=jnp.float32).at[slot_owner].max(part_lse)
    peak = jnp.maximum(peak, tail_lse)
    scaled = jnp.exp(part_lse - peak[slot_owner])
    numer = jnp.zeros(tail_part.shape, jnp.float32).at[slot_owner].add(scaled[..., None] * parts)
    denom = jnp.zeros(tail_lse.shape, jnp.float32).at[slot_owner].add(scaled)
    tail_w = jnp.exp(tail_lse - peak)
    final = (numer + tail_w[..., None] * tail_part) / (denom + tail_w)[..., None]
    final = jnp.transpose(final, (2, 0, 1, 3, 4)).reshape(STEPS, REQUESTS, HEADS_Q * HEAD_DIM)
    return final.astype(jnp.bfloat16)
```

```python
import math

import jax
import jax.numpy as jnp
from jax import lax
from jax.experimental import pallas as pl
from jax.experimental.pallas import tpu as pltpu
from jax.sharding import PartitionSpec as P

BLOCK = 2048
WIDTH = 128
ROWS = 64
NX, NZ, NC, NY = 4, 16, 2, 4
GROUPS = NX * NC
SLOTS = 4
SCALE = 1.0 / math.sqrt(WIDTH)
NEG = -1e30
F32 = jnp.float32
BF16 = jnp.bfloat16

HOPS = (6, -6, 2, -2)
NEXT = {6: (-1, 1, 2), -6: (1, -1), 2: (-1, 1, 2), -2: (1, -1, -2)}
FORWARD = [(d, f) for d in HOPS for f in NEXT[d]]
ROW_PEERS = [(dx, dc) for dx in range(NX) for dc in range(NC)][1:]


def kernel(
    q_ref, fresh_ref, kv_ref, len_ref, owner_ref, block_ref, out_ref,
    kv, qall, rowtab, ivec, tab_s, ivec_s, sel, got, parts, lses, lrow, wmat, wcol,
    cbuf, clse, rbuf, rlse, mbuf, mlse, fbuf, flse, tail, tail_lse,
    kv_sem, y_ss, y_rs, t_ss, t_rs, sm_sem, a_ss, a_rs, b_ss, b_rs, s_ss, s_rs,
    p_ss, p_rs, l_ss, l_rs, c_ss, c_rs, d_ss, d_rs, e_ss, e_rs, f_ss, f_rs,
):
    me = lax.axis_index("inst")
    y = lax.axis_index("tp")
    x, z, c = me // (NZ * NC), (me // NC) % NZ, me % NC
    g = x * NC + c

    def at(dx, dz, dc, dy):
        xx, zz = (x + dx + NX) % NX, (z + dz + NZ) % NZ
        cc, yy = (c + dc) % NC, (y + dy) % NY
        return ((xx * NZ + zz) * NC + cc, yy)

    def send(src, dst, ss, rs, to):
        return pltpu.make_async_remote_copy(
            src_ref=src, dst_ref=dst, send_sem=ss, recv_sem=rs,
            device_id=to, device_id_type=pl.DeviceIdType.MESH,
        )

    peers = [at(0, d, 0, 0) for d in (6, -6, 2, -2, 1, -1)]
    peers += [at(dx, 0, dc, 0) for dx, dc in ROW_PEERS]
    peers += [at(0, 0, 0, d) for d in range(1, NY)]
    barrier = pltpu.get_barrier_semaphore()
    for p in peers:
        pl.semaphore_signal(barrier, inc=1, device_id=p, device_id_type=pl.DeviceIdType.MESH)
    kv_copies = [pltpu.make_async_copy(kv_ref.at[s], kv.at[s], kv_sem.at[s]) for s in range(SLOTS)]
    for copy in kv_copies:
        copy.start()
    row = lax.broadcasted_iota(jnp.int32, (16, WIDTH), 0) % 4
    hi = jnp.where(row < 2, len_ref[0] // 64, len_ref[1] // 64)
    lo = jnp.where(row < 2, len_ref[0] % 64, len_ref[1] % 64)
    qall[z, 0:8] = q_ref[...]
    qall[z, 8] = jnp.where(row % 2 == 0, hi, lo).astype(F32).astype(BF16)
    rowtab[g, y] = jnp.full((1, WIDTH), owner_ref[0] * 4 + block_ref[0], jnp.int32)
    pl.semaphore_wait(barrier, len(peers))

    first = {
        d: send(qall.at[z], qall.at[z], a_ss.at[i], a_rs.at[i], at(0, d, 0, 0))
        for i, d in enumerate(HOPS)
    }
    for d in HOPS:
        first[d].start()
    tables = []
    for i in range(NY - 1):
        tables.append(send(rowtab.at[g, y], rowtab.at[g, y], y_ss.at[i], y_rs.at[i], at(0, 0, 0, i + 1)))
        tables[-1].start()

    for r in range(2):
        qf = q_ref[4 * r : 4 * r + 4].reshape(ROWS, WIDTH).astype(F32)
        step = lax.broadcasted_iota(jnp.int32, (ROWS, 1), 0) // 16
        ss = []
        for b in range(4):
            k_b = fresh_ref[b].astype(F32)[r : r + 1, :WIDTH]
            s_b = jnp.sum(qf * k_b, axis=1, keepdims=True) * SCALE
            ss.append(jnp.where(step >= b, s_b, -jnp.inf))
        top = jnp.maximum(jnp.maximum(ss[0], ss[1]), jnp.maximum(ss[2], ss[3]))
        ws = [jnp.exp(s_b - top) for s_b in ss]
        total = ws[0] + ws[1] + ws[2] + ws[3]
        acc = jnp.zeros((ROWS, WIDTH), F32)
        for b in range(4):
            v_b = fresh_ref[b].astype(F32)[r : r + 1, WIDTH:]
            acc = acc + ws[b].astype(BF16).astype(F32) * v_b
        tail[r] = acc / total
        tail_lse[r] = jnp.broadcast_to(top + jnp.log(total), (ROWS, WIDTH))

    for t in tables:
        t.wait_recv()
    rows = []
    for i, (dx, dc) in enumerate(ROW_PEERS):
        rows.append(send(rowtab.at[g], rowtab.at[g], t_ss.at[i], t_rs.at[i], at(dx, 0, dc, 0)))
        rows[-1].start()

    second = []
    for d in (2, -2, 6, -6):
        first[d].wait_recv()
        came = (z - d + NZ) % NZ
        for j, (dd, f) in enumerate(FORWARD):
            if dd == d:
                second.append(send(qall.at[came], qall.at[came], b_ss.at[j], b_rs.at[j], at(0, f, 0, 0)))
                second[-1].start()

    for t in rows:
        t.wait_recv()
    lane = lax.broadcasted_iota(jnp.int32, (1, WIDTH), 1)
    want = (((x * NZ + (lane % 32) // 2) * NC + c) * 2 + lane % 2) * 4 + lane // 32
    index = jnp.zeros((1, WIDTH), jnp.int32)
    count = jnp.zeros((1, WIDTH), jnp.int32)
    for gg in range(GROUPS):
        for s in range(SLOTS):
            hit = rowtab[gg, s] == want
            index = jnp.where(hit, gg * SLOTS + s, index)
            count = jnp.where(hit, 1, count)
    ivec[0] = index
    ivec[1] = count
    to_smem = [
        pltpu.make_async_copy(rowtab, tab_s, sm_sem.at[0]),
        pltpu.make_async_copy(ivec, ivec_s, sm_sem.at[1]),
    ]
    for copy in to_smem:
        copy.start()
    for copy in to_smem:
        copy.wait()

    for t in second:
        t.wait_recv()

    group = lax.broadcasted_iota(jnp.int32, (16, WIDTH), 0) // 4

    def choose(gg, put):
        lens = jnp.zeros((16, WIDTH), BF16)
        for s in range(SLOTS):
            owner = tab_s[gg, s, 0, 0] // 4
            zz, r = (owner // 4) % NZ, owner % 2
            put(slice(4 * s, 4 * s + 4), qall[zz, pl.ds(4 * r, 4)])
            lens = jnp.where(group == s, qall[zz, 8].astype(F32), lens.astype(F32)).astype(BF16)
        put(16, lens)

    queries = []
    for i, (dx, dc) in enumerate(ROW_PEERS):
        gg = ((x + dx) % NX) * NC + (c + dc) % NC

        def put(k, v, i=i):
            sel[i, k] = v

        choose(gg, put)
        queries.append(send(sel.at[i], got.at[g], s_ss.at[i], s_rs.at[i], at(dx, 0, dc, 0)))
        queries[-1].start()

    def put_own(k, v):
        got[g, k] = v

    choose(g, put_own)
    for copy in kv_copies:
        copy.wait()
    for t in queries:
        t.wait_recv()

    lane_pos = lax.broadcasted_iota(jnp.int32, (1, BLOCK), 1).astype(F32)
    lane_id = lax.broadcasted_iota(jnp.int32, (ROWS, WIDTH), 1)
    lcols = jnp.zeros((ROWS, WIDTH), F32)
    back = []
    for s in range(SLOTS):
        code = tab_s[g, s, 0, 0]
        owner, blk = code // 4, code % 4
        src = (owner // 64) * NC + (owner // 2) % NC
        r = owner % 2
        q = got[src, pl.ds(4 * s, 4)].reshape(ROWS, WIDTH)
        lens = got[src, 16].astype(F32)
        hi = jnp.where(r == 0, lens[4 * s : 4 * s + 1], lens[4 * s + 2 : 4 * s + 3])
        lo = jnp.where(r == 0, lens[4 * s + 1 : 4 * s + 2], lens[4 * s + 3 : 4 * s + 4])
        left = (hi * 64.0 + lo)[:, :1] - (blk * BLOCK).astype(F32)
        scores = lax.dot_general(
            q, kv[s, :, :WIDTH], (((1,), (1,)), ((), ())), preferred_element_type=F32
        ) * SCALE
        scores = jnp.where(lane_pos < left, scores, -jnp.inf)
        top = jnp.max(scores, axis=1, keepdims=True)
        weights = jnp.exp(scores - top)
        total = jnp.sum(weights, axis=1, keepdims=True)
        part = jnp.dot(weights.astype(BF16), kv[s, :, WIDTH:], preferred_element_type=F32) / total
        parts[g, s] = part.astype(BF16).reshape(4, 16, WIDTH)
        lcols = jnp.where(lane_id == s, top + jnp.log(total), lcols)
        for i, (dx, dc) in enumerate(ROW_PEERS):
            copy = send(parts.at[g, s], parts.at[g, s], p_ss.at[i, s], p_rs.at[i, s], at(dx, 0, dc, 0))
            copy.start()
            back.append(copy)
    lt = jnp.concatenate([lcols, lcols], axis=0).T
    for s in range(SLOTS):
        lses[g, s] = lt[s : s + 1]
    for i, (dx, dc) in enumerate(ROW_PEERS):
        copy = send(lses.at[g], lses.at[g], l_ss.at[i], l_rs.at[i], at(dx, 0, dc, 0))
        copy.start()
        back.append(copy)
    for copy in back:
        copy.wait_recv()

    half = lax.broadcasted_iota(jnp.int32, (1, WIDTH), 1) < ROWS
    wmat[...] = jnp.zeros((WIDTH, WIDTH), F32)

    def where_is(d, r, k):
        j = k * 32 + ((z + d) % NZ) * 2 + r
        return ivec_s[0, 0, j], ivec_s[1, 0, j]

    for d in range(NZ):
        for k in range(3):
            pair = []
            for r in range(2):
                i, n = where_is(d, r, k)
                pair.append(jnp.where(n > 0, lses[i // 4, i % 4], NEG))
            lrow[k, d] = jnp.where(half, pair[0], pair[1])[0]
    l0, l1, l2 = lrow[0], lrow[1], lrow[2]
    peak = jnp.maximum(jnp.maximum(l0, l1), l2)
    w0, w1, w2 = jnp.exp(l0 - peak), jnp.exp(l1 - peak), jnp.exp(l2 - peak)
    total = w0 + w1 + w2
    merged = peak + jnp.log(total)
    wmat[0:16] = w0 / total
    wmat[16:32] = w1 / total
    wmat[32:48] = w2 / total
    for d in range(NZ):
        clse[d] = merged[d : d + 1]
    wcol[...] = wmat[...].T

    def build(d):
        d = d % NZ
        for r in range(2):
            acc = jnp.zeros((ROWS, WIDTH), F32)
            for k in range(3):
                i, _ = where_is(d, r, k)
                p = parts[i // 4, i % 4].reshape(ROWS, WIDTH).astype(F32)
                acc = acc + wcol[r * ROWS : (r + 1) * ROWS, k * 16 + d : k * 16 + d + 1] * p
            cbuf[d, 4 * r : 4 * r + 4] = acc.astype(BF16).reshape(4, 16, WIDTH)

    relayed = []
    for j, (dd, f) in enumerate(FORWARD):
        e = (-f - dd) % NZ
        build(e)
        relayed.append(
            (
                send(cbuf.at[e], rbuf.at[j], c_ss.at[j], c_rs.at[j], at(0, -f, 0, 0)),
                send(clse.at[e], rlse.at[j], d_ss.at[j], d_rs.at[j], at(0, -f, 0, 0)),
            )
        )
        for copy in relayed[-1]:
            copy.start()
    for d in HOPS:
        build(-d)
    build(0)
    final = []
    for i, d in enumerate(HOPS):
        js = [j for j, (dd, _) in enumerate(FORWARD) if dd == d]
        for j in js:
            for copy in relayed[j]:
                copy.wait_recv()
        ls = [clse[(-d) % NZ]] + [rlse[j] for j in js]
        peak = ls[0]
        for l in ls[1:]:
            peak = jnp.maximum(peak, l)
        ws = [jnp.exp(l - peak) for l in ls]
        total = ws[0]
        for w in ws[1:]:
            total = total + w
        mlse[i] = peak + jnp.log(total)
        for n, w in enumerate(ws):
            wmat[n : n + 1] = w / total
        wt = wmat[...].T
        data = [cbuf[(-d) % NZ]] + [rbuf[j] for j in js]
        acc = jnp.zeros((WIDTH, WIDTH), F32)
        for n, p in enumerate(data):
            acc = acc + wt[:, n : n + 1] * p.reshape(WIDTH, WIDTH).astype(F32)
        mbuf[i] = acc.astype(BF16).reshape(8, 16, WIDTH)
        final.append(
            (
                send(mbuf.at[i], fbuf.at[i], e_ss.at[i], e_rs.at[i], at(0, -d, 0, 0)),
                send(mlse.at[i], flse.at[i], f_ss.at[i], f_rs.at[i], at(0, -d, 0, 0)),
            )
        )
        for copy in final[-1]:
            copy.start()
    for pair in final:
        for copy in pair:
            copy.wait_recv()
    for i in range(4):
        wmat[i : i + 1] = flse[i]
    wmat[4:5] = clse[0]
    wt = wmat[...].T
    for r in range(2):
        rs = slice(r * ROWS, (r + 1) * ROWS)
        tl = tail_lse[r][:, :1]
        ls = [wt[rs, n : n + 1] for n in range(5)]
        peak = tl
        for l in ls:
            peak = jnp.maximum(peak, l)
        w = jnp.exp(tl - peak)
        denom = w
        acc = w * tail[r]
        for n in range(5):
            p = cbuf[0, 4 * r : 4 * r + 4] if n == 4 else fbuf[n, 4 * r : 4 * r + 4]
            w = jnp.exp(ls[n] - peak)
            denom = denom + w
            acc = acc + w * p.reshape(ROWS, WIDTH).astype(F32)
        out_ref[4 * r : 4 * r + 4] = (acc / denom).astype(BF16).reshape(4, 16, WIDTH)

    for copy in list(first.values()) + tables + rows + second + queries + back:
        copy.wait_send()
    for pair in relayed + final:
        for copy in pair:
            copy.wait_send()


def shards(query, fresh_key_value, kv_pool, lengths, slot_owner, slot_block):
    steps, req_dev, width = query.shape
    q = jnp.transpose(query.reshape(steps, req_dev, 16, WIDTH), (1, 0, 2, 3)).reshape(8, 16, WIDTH)
    dma = pltpu.SemaphoreType.DMA
    vmem, smem = pl.BlockSpec(memory_space=pltpu.VMEM), pl.BlockSpec(memory_space=pltpu.SMEM)
    n, m = len(ROW_PEERS), len(FORWARD)
    out = pl.pallas_call(
        kernel,
        out_shape=jax.ShapeDtypeStruct((8, 16, WIDTH), BF16),
        in_specs=[vmem, vmem, pl.BlockSpec(memory_space=pl.ANY), smem, smem, smem],
        out_specs=vmem,
        scratch_shapes=[
            pltpu.VMEM((SLOTS, BLOCK, 2 * WIDTH), BF16),
            pltpu.VMEM((NZ, 9, 16, WIDTH), BF16),
            pltpu.VMEM((GROUPS, SLOTS, 1, WIDTH), jnp.int32),
            pltpu.VMEM((2, 1, WIDTH), jnp.int32),
            pltpu.SMEM((GROUPS, SLOTS, 1, WIDTH), jnp.int32),
            pltpu.SMEM((2, 1, WIDTH), jnp.int32),
            pltpu.VMEM((n, 17, 16, WIDTH), BF16),
            pltpu.VMEM((GROUPS, 17, 16, WIDTH), BF16),
            pltpu.VMEM((GROUPS, SLOTS, 4, 16, WIDTH), BF16),
            pltpu.VMEM((GROUPS, SLOTS, 1, WIDTH), F32),
            pltpu.VMEM((3, NZ, WIDTH), F32),
            pltpu.VMEM((WIDTH, WIDTH), F32),
            pltpu.VMEM((WIDTH, WIDTH), F32),
            pltpu.VMEM((NZ, 8, 16, WIDTH), BF16),
            pltpu.VMEM((NZ, 1, WIDTH), F32),
            pltpu.VMEM((m, 8, 16, WIDTH), BF16),
            pltpu.VMEM((m, 1, WIDTH), F32),
            pltpu.VMEM((4, 8, 16, WIDTH), BF16),
            pltpu.VMEM((4, 1, WIDTH), F32),
            pltpu.VMEM((4, 8, 16, WIDTH), BF16),
            pltpu.VMEM((4, 1, WIDTH), F32),
            pltpu.VMEM((2, ROWS, WIDTH), F32),
            pltpu.VMEM((2, ROWS, WIDTH), F32),
            dma((SLOTS,)),
            dma((3,)), dma((3,)),
            dma((n,)), dma((n,)),
            dma((2,)),
            dma((4,)), dma((4,)),
            dma((m,)), dma((m,)),
            dma((n,)), dma((n,)),
            dma((n, SLOTS)), dma((n, SLOTS)),
            dma((n,)), dma((n,)),
            dma((m,)), dma((m,)),
            dma((m,)), dma((m,)),
            dma((4,)), dma((4,)),
            dma((4,)), dma((4,)),
        ],
        compiler_params=pltpu.CompilerParams(
            collective_id=0, has_side_effects=True, vmem_limit_bytes=40 << 20
        ),
        name="lent_attention",
    )(q, fresh_key_value, kv_pool, lengths, slot_owner, slot_block)
    out = jnp.transpose(out.reshape(req_dev, steps, 16, WIDTH), (1, 0, 2, 3))
    return out.reshape(steps, req_dev, width)


def solution(mesh):
    placed = (
        P(None, "inst", "tp"),
        P(None, "inst", "tp"),
        P("inst", None, "tp"),
        P("inst"),
        P(("inst", "tp")),
        P(("inst", "tp")),
    )
    return jax.shard_map(
        shards, mesh=mesh, in_specs=placed, out_specs=P(None, "inst", "tp"), check_vma=False
    )
```

```python
import math

import jax
import jax.numpy as jnp
from jax import lax
from jax.experimental import pallas as pl
from jax.experimental.pallas import tpu as pltpu
from jax.sharding import PartitionSpec as P

BLOCK = 2048
WIDTH = 128
ROWS = 64
NX, NZ, NC, NY = 4, 16, 2, 4
GROUPS = NX * NC
SLOTS = 4
SCALE = 1.0 / math.sqrt(WIDTH)
NEG = -1e30
F32 = jnp.float32
BF16 = jnp.bfloat16

HOPS = (5, -5, 2, -2)
NEXT = {5: (1, 2, 3), -5: (-1, -2), 2: (-1, 1, 2), -2: (1, -1, -2)}
FORWARD = [(d, f) for d in HOPS for f in NEXT[d]]
ROW_PEERS = [(dx, dc) for dx in range(NX) for dc in range(NC)][1:]
GATHER = ((1, 0), (3, 0), (2, 0), (0, 1))


def kernel(
    q_in, fresh_in, kv_ref, len_in, owner_in, block_in, out_ref,
    q_raw, q_ref, fresh_ref, len_ref, owner_ref, block_ref,
    kv, qall, rowtab, ivec, tab_s, ivec_s, sel, got0, got1, parts, lses, lrow, wmat, wcol,
    cbuf, clse, rbuf, rlse, mbuf, mlse, fbuf, flse, tail, tail_lse,
    in_sem, kv_sem, y_ss, y_rs, t_ss, t_rs, sm_sem, a_ss, a_rs, b_ss, b_rs, s_ss, s_rs,
    p_ss, p_rs, l_ss, l_rs, u_ss, u_rs, v_ss, v_rs, c_ss, c_rs, d_ss, d_rs, e_ss, e_rs, f_ss, f_rs,
):
    me = lax.axis_index("inst")
    y = lax.axis_index("tp")
    x, z, c = me // (NZ * NC), (me // NC) % NZ, me % NC
    g = x * NC + c

    def at(dx, dz, dc, dy):
        xx, zz = (x + dx + NX) % NX, (z + dz + NZ) % NZ
        cc, yy = (c + dc) % NC, (y + dy) % NY
        return ((xx * NZ + zz) * NC + cc, yy)

    def send(src, dst, ss, rs, to):
        return pltpu.make_async_remote_copy(
            src_ref=src, dst_ref=dst, send_sem=ss, recv_sem=rs,
            device_id=to, device_id_type=pl.DeviceIdType.MESH,
        )

    peers = [at(0, d, 0, 0) for d in (5, -5, 3, -3, 2, -2, 1, -1)]
    peers += [at(dx, 0, dc, 0) for dx, dc in ROW_PEERS]
    peers += [at(0, 0, 0, d) for d in range(1, NY)]
    barrier = pltpu.get_barrier_semaphore()
    for p in peers:
        pl.semaphore_signal(barrier, inc=1, device_id=p, device_id_type=pl.DeviceIdType.MESH)
    inputs = [
        pltpu.make_async_copy(a, b, in_sem.at[i])
        for i, (a, b) in enumerate(
            ((q_in, q_raw), (len_in, len_ref), (owner_in, owner_ref), (block_in, block_ref), (fresh_in, fresh_ref))
        )
    ]
    for copy in inputs:
        copy.start()
    kv_copies = [pltpu.make_async_copy(kv_ref.at[s], kv.at[s], kv_sem.at[s]) for s in range(SLOTS)]
    for copy in kv_copies:
        copy.start()
    for copy in inputs:
        copy.wait()
    for a in range(4):
        qa = q_raw[a].astype(F32)
        for r in range(2):
            tile = jnp.concatenate([qa[r : r + 1, WIDTH * h : WIDTH * (h + 1)] for h in range(16)], axis=0)
            q_ref[4 * r + a] = tile.astype(BF16)
    row = lax.broadcasted_iota(jnp.int32, (16, WIDTH), 0) % 4
    hi = jnp.where(row < 2, len_ref[0] // 64, len_ref[1] // 64)
    lo = jnp.where(row < 2, len_ref[0] % 64, len_ref[1] % 64)
    qall[z, 0:8] = q_ref[...]
    qall[z, 8] = jnp.where(row % 2 == 0, hi, lo).astype(F32).astype(BF16)
    rowtab[g, y] = jnp.full((1, WIDTH), owner_ref[0] * 4 + block_ref[0], jnp.int32)
    pl.semaphore_wait(barrier, len(peers))

    first = {
        d: send(qall.at[z], qall.at[z], a_ss.at[i], a_rs.at[i], at(0, d, 0, 0))
        for i, d in enumerate(HOPS)
    }
    for d in HOPS:
        first[d].start()
    tables = []
    for i in range(NY - 1):
        tables.append(send(rowtab.at[g, y], rowtab.at[g, y], y_ss.at[i], y_rs.at[i], at(0, 0, 0, i + 1)))
        tables[-1].start()

    for r in range(2):
        qf = q_ref[4 * r : 4 * r + 4].reshape(ROWS, WIDTH).astype(F32)
        step = lax.broadcasted_iota(jnp.int32, (ROWS, 1), 0) // 16
        ss = []
        for b in range(4):
            k_b = fresh_ref[b].astype(F32)[r : r + 1, :WIDTH]
            s_b = jnp.sum(qf * k_b, axis=1, keepdims=True) * SCALE
            ss.append(jnp.where(step >= b, s_b, -jnp.inf))
        top = jnp.maximum(jnp.maximum(ss[0], ss[1]), jnp.maximum(ss[2], ss[3]))
        ws = [jnp.exp(s_b - top) for s_b in ss]
        total = ws[0] + ws[1] + ws[2] + ws[3]
        acc = jnp.zeros((ROWS, WIDTH), F32)
        for b in range(4):
            v_b = fresh_ref[b].astype(F32)[r : r + 1, WIDTH:]
            acc = acc + ws[b].astype(BF16).astype(F32) * v_b
        tail[r] = acc / total
        tail_lse[r] = jnp.broadcast_to(top + jnp.log(total), (ROWS, WIDTH))

    for t in tables:
        t.wait_recv()
    rows = []
    for i, (dx, dc) in enumerate(ROW_PEERS):
        rows.append(send(rowtab.at[g], rowtab.at[g], t_ss.at[i], t_rs.at[i], at(dx, 0, dc, 0)))
        rows[-1].start()

    second = []
    for d in (2, -2, 5, -5):
        first[d].wait_recv()
        came = (z - d + NZ) % NZ
        for j, (dd, f) in enumerate(FORWARD):
            if dd == d:
                second.append(send(qall.at[came], qall.at[came], b_ss.at[j], b_rs.at[j], at(0, f, 0, 0)))
                second[-1].start()

    for t in rows:
        t.wait_recv()
    lane = lax.broadcasted_iota(jnp.int32, (1, WIDTH), 1)
    want = (((x * NZ + (lane % 32) // 2) * NC + c) * 2 + lane % 2) * 4 + lane // 32
    index = jnp.zeros((1, WIDTH), jnp.int32)
    count = jnp.zeros((1, WIDTH), jnp.int32)
    for gg in range(GROUPS):
        for s in range(SLOTS):
            hit = rowtab[gg, s] == want
            index = jnp.where(hit, gg * SLOTS + s, index)
            count = jnp.where(hit, 1, count)
    ivec[0] = index
    ivec[1] = count
    to_smem = [
        pltpu.make_async_copy(rowtab, tab_s, sm_sem.at[0]),
        pltpu.make_async_copy(ivec, ivec_s, sm_sem.at[1]),
    ]
    for copy in to_smem:
        copy.start()
    for copy in to_smem:
        copy.wait()

    for t in second:
        t.wait_recv()

    group = lax.broadcasted_iota(jnp.int32, (16, WIDTH), 0) // 4

    got = (got0, got1)

    def choose(gg, half, ref):
        lens = jnp.zeros((16, WIDTH), F32)
        for i in range(2):
            owner = tab_s[gg, 2 * half + i, 0, 0] // 4
            zz, r = (owner // 4) % NZ, owner % 2
            ref[4 * i : 4 * i + 4] = qall[zz, pl.ds(4 * r, 4)]
            lens = jnp.where(group == i, qall[zz, 8].astype(F32), lens)
        ref[8] = lens.astype(BF16)

    queries = []
    for half in range(2):
        for i, (dx, dc) in enumerate(ROW_PEERS):
            gg = ((x + dx) % NX) * NC + (c + dc) % NC
            choose(gg, half, sel.at[i, half])
            copy = send(
                sel.at[i, half], got[half].at[g], s_ss.at[i, half], s_rs.at[i, half], at(dx, 0, dc, 0)
            )
            copy.start()
            queries.append(copy)
        choose(g, half, got[half].at[g])
    for copy in kv_copies:
        copy.wait()

    lane_pos = lax.broadcasted_iota(jnp.int32, (1, BLOCK), 1).astype(F32)
    lane_id = lax.broadcasted_iota(jnp.int32, (ROWS, WIDTH), 1)
    lcols = jnp.zeros((ROWS, WIDTH), F32)
    back = []
    for half in range(2):
        for t in queries[half * len(ROW_PEERS) : (half + 1) * len(ROW_PEERS)]:
            t.wait_recv()
        for n in range(2):
            s = 2 * half + n
            code = tab_s[g, s, 0, 0]
            owner, blk = code // 4, code % 4
            src = (owner // 64) * NC + (owner // 2) % NC
            r = owner % 2
            q = got[half][src, 4 * n : 4 * n + 4].reshape(ROWS, WIDTH)
            lens = got[half][src, 8].astype(F32)
            hi = jnp.where(r == 0, lens[4 * n : 4 * n + 1], lens[4 * n + 2 : 4 * n + 3])
            lo = jnp.where(r == 0, lens[4 * n + 1 : 4 * n + 2], lens[4 * n + 3 : 4 * n + 4])
            left = (hi * 64.0 + lo)[:, :1] - (blk * BLOCK).astype(F32)
            scores = lax.dot_general(
                q, kv[s, :, :WIDTH], (((1,), (1,)), ((), ())), preferred_element_type=F32
            ) * SCALE
            scores = jnp.where(lane_pos < left, scores, -jnp.inf)
            top = jnp.max(scores, axis=1, keepdims=True)
            weights = jnp.exp(scores - top)
            total = jnp.sum(weights, axis=1, keepdims=True)
            part = jnp.dot(weights.astype(BF16), kv[s, :, WIDTH:], preferred_element_type=F32) / total
            parts[g, s] = part.astype(BF16).reshape(4, 16, WIDTH)
            lcols = jnp.where(lane_id == s, top + jnp.log(total), lcols)
        mine = parts.at[g, 2 * half : 2 * half + 2]
        for i, (dx, dc) in enumerate(GATHER):
            copy = send(mine, mine, p_ss.at[i, half], p_rs.at[i, half], at(dx, 0, dc, 0))
            copy.start()
            back.append(copy)
    lt = jnp.concatenate([lcols, lcols], axis=0).T
    for s in range(SLOTS):
        lses[g, s] = lt[s : s + 1]
    lse_sent = []
    for i, (dx, dc) in enumerate(GATHER):
        copy = send(lses.at[g], lses.at[g], l_ss.at[i], l_rs.at[i], at(dx, 0, dc, 0))
        copy.start()
        lse_sent.append(copy)
    handed = []
    for half in range(2):
        for i, (dx, _) in enumerate(GATHER[:3]):
            back[half * len(GATHER) + i].wait_recv()
            there = parts.at[((x - dx + NX) % NX) * NC + c, 2 * half : 2 * half + 2]
            copy = send(there, there, u_ss.at[i, half], u_rs.at[i, half], at(0, 0, 1, 0))
            copy.start()
            handed.append(copy)
    for i, (dx, _) in enumerate(GATHER[:3]):
        lse_sent[i].wait_recv()
        there = lses.at[((x - dx + NX) % NX) * NC + c]
        copy = send(there, there, v_ss.at[i], v_rs.at[i], at(0, 0, 1, 0))
        copy.start()
        handed.append(copy)
    for half in range(2):
        back[half * len(GATHER) + 3].wait_recv()
    lse_sent[3].wait_recv()
    for copy in handed:
        copy.wait_recv()
    back = back + lse_sent + handed

    half = lax.broadcasted_iota(jnp.int32, (1, WIDTH), 1) < ROWS
    wmat[...] = jnp.zeros((WIDTH, WIDTH), F32)

    def where_is(d, r, k):
        j = k * 32 + ((z + d) % NZ) * 2 + r
        return ivec_s[0, 0, j], ivec_s[1, 0, j]

    for d in range(NZ):
        for k in range(3):
            pair = []
            for r in range(2):
                i, n = where_is(d, r, k)
                pair.append(jnp.where(n > 0, lses[i // 4, i % 4], NEG))
            lrow[k, d] = jnp.where(half, pair[0], pair[1])[0]
    l0, l1, l2 = lrow[0], lrow[1], lrow[2]
    peak = jnp.maximum(jnp.maximum(l0, l1), l2)
    w0, w1, w2 = jnp.exp(l0 - peak), jnp.exp(l1 - peak), jnp.exp(l2 - peak)
    total = w0 + w1 + w2
    merged = peak + jnp.log(total)
    wmat[0:16] = w0 / total
    wmat[16:32] = w1 / total
    wmat[32:48] = w2 / total
    for d in range(NZ):
        clse[d] = merged[d : d + 1]
    wcol[...] = wmat[...].T

    def build(d):
        d = d % NZ
        for r in range(2):
            acc = jnp.zeros((ROWS, WIDTH), F32)
            for k in range(3):
                i, _ = where_is(d, r, k)
                p = parts[i // 4, i % 4].reshape(ROWS, WIDTH).astype(F32)
                acc = acc + wcol[r * ROWS : (r + 1) * ROWS, k * 16 + d : k * 16 + d + 1] * p
            cbuf[d, 4 * r : 4 * r + 4] = acc.astype(BF16).reshape(4, 16, WIDTH)

    relayed = []
    for j, (dd, f) in enumerate(FORWARD):
        e = (-f - dd) % NZ
        build(e)
        relayed.append(
            (
                send(cbuf.at[e], rbuf.at[j], c_ss.at[j], c_rs.at[j], at(0, -f, 0, 0)),
                send(clse.at[e], rlse.at[j], d_ss.at[j], d_rs.at[j], at(0, -f, 0, 0)),
            )
        )
        for copy in relayed[-1]:
            copy.start()
    for d in HOPS:
        build(-d)
    build(0)
    final = []
    for i, d in enumerate(HOPS):
        js = [j for j, (dd, _) in enumerate(FORWARD) if dd == d]
        for j in js:
            for copy in relayed[j]:
                copy.wait_recv()
        ls = [clse[(-d) % NZ]] + [rlse[j] for j in js]
        peak = ls[0]
        for l in ls[1:]:
            peak = jnp.maximum(peak, l)
        ws = [jnp.exp(l - peak) for l in ls]
        total = ws[0]
        for w in ws[1:]:
            total = total + w
        mlse[i] = peak + jnp.log(total)
        for n, w in enumerate(ws):
            wmat[n : n + 1] = w / total
        wt = wmat[...].T
        data = [cbuf[(-d) % NZ]] + [rbuf[j] for j in js]
        acc = jnp.zeros((WIDTH, WIDTH), F32)
        for n, p in enumerate(data):
            acc = acc + wt[:, n : n + 1] * p.reshape(WIDTH, WIDTH).astype(F32)
        mbuf[i] = acc.astype(BF16).reshape(8, 16, WIDTH)
        final.append(
            (
                send(mbuf.at[i], fbuf.at[i], e_ss.at[i], e_rs.at[i], at(0, -d, 0, 0)),
                send(mlse.at[i], flse.at[i], f_ss.at[i], f_rs.at[i], at(0, -d, 0, 0)),
            )
        )
        for copy in final[-1]:
            copy.start()
    for pair in final:
        for copy in pair:
            copy.wait_recv()
    for i in range(4):
        wmat[i : i + 1] = flse[i]
    wmat[4:5] = clse[0]
    wt = wmat[...].T
    for r in range(2):
        rs = slice(r * ROWS, (r + 1) * ROWS)
        tl = tail_lse[r][:, :1]
        ls = [wt[rs, n : n + 1] for n in range(5)]
        peak = tl
        for l in ls:
            peak = jnp.maximum(peak, l)
        w = jnp.exp(tl - peak)
        denom = w
        acc = w * tail[r]
        for n in range(5):
            p = cbuf[0, 4 * r : 4 * r + 4] if n == 4 else fbuf[n, 4 * r : 4 * r + 4]
            w = jnp.exp(ls[n] - peak)
            denom = denom + w
            acc = acc + w * p.reshape(ROWS, WIDTH).astype(F32)
        out_ref[4 * r : 4 * r + 4] = (acc / denom).astype(BF16).reshape(4, 16, WIDTH)

    for copy in list(first.values()) + tables + rows + second + queries + back:
        copy.wait_send()
    for pair in relayed + final:
        for copy in pair:
            copy.wait_send()


def shards(query, fresh_key_value, kv_pool, lengths, slot_owner, slot_block):
    steps, req_dev, width = query.shape
    dma = pltpu.SemaphoreType.DMA
    hbm = pl.BlockSpec(memory_space=pl.ANY)
    n, m = len(ROW_PEERS), len(FORWARD)
    out = pl.pallas_call(
        kernel,
        out_shape=jax.ShapeDtypeStruct((8, 16, WIDTH), BF16),
        in_specs=[hbm] * 6,
        out_specs=pl.BlockSpec(memory_space=pltpu.VMEM),
        scratch_shapes=[
            pltpu.VMEM(query.shape, BF16),
            pltpu.VMEM((8, 16, WIDTH), BF16),
            pltpu.VMEM(fresh_key_value.shape, BF16),
            pltpu.SMEM(lengths.shape, jnp.int32),
            pltpu.SMEM(slot_owner.shape, jnp.int32),
            pltpu.SMEM(slot_block.shape, jnp.int32),
            pltpu.VMEM((SLOTS, BLOCK, 2 * WIDTH), BF16),
            pltpu.VMEM((NZ, 9, 16, WIDTH), BF16),
            pltpu.VMEM((GROUPS, SLOTS, 1, WIDTH), jnp.int32),
            pltpu.VMEM((2, 1, WIDTH), jnp.int32),
            pltpu.SMEM((GROUPS, SLOTS, 1, WIDTH), jnp.int32),
            pltpu.SMEM((2, 1, WIDTH), jnp.int32),
            pltpu.VMEM((n, 2, 9, 16, WIDTH), BF16),
            pltpu.VMEM((GROUPS, 9, 16, WIDTH), BF16),
            pltpu.VMEM((GROUPS, 9, 16, WIDTH), BF16),
            pltpu.VMEM((GROUPS, SLOTS, 4, 16, WIDTH), BF16),
            pltpu.VMEM((GROUPS, SLOTS, 1, WIDTH), F32),
            pltpu.VMEM((3, NZ, WIDTH), F32),
            pltpu.VMEM((WIDTH, WIDTH), F32),
            pltpu.VMEM((WIDTH, WIDTH), F32),
            pltpu.VMEM((NZ, 8, 16, WIDTH), BF16),
            pltpu.VMEM((NZ, 1, WIDTH), F32),
            pltpu.VMEM((m, 8, 16, WIDTH), BF16),
            pltpu.VMEM((m, 1, WIDTH), F32),
            pltpu.VMEM((4, 8, 16, WIDTH), BF16),
            pltpu.VMEM((4, 1, WIDTH), F32),
            pltpu.VMEM((4, 8, 16, WIDTH), BF16),
            pltpu.VMEM((4, 1, WIDTH), F32),
            pltpu.VMEM((2, ROWS, WIDTH), F32),
            pltpu.VMEM((2, ROWS, WIDTH), F32),
            dma((5,)),
            dma((SLOTS,)),
            dma((3,)), dma((3,)),
            dma((n,)), dma((n,)),
            dma((2,)),
            dma((4,)), dma((4,)),
            dma((m,)), dma((m,)),
            dma((n, 2)), dma((n, 2)),
            dma((4, 2)), dma((4, 2)),
            dma((4,)), dma((4,)),
            dma((3, 2)), dma((3, 2)),
            dma((3,)), dma((3,)),
            dma((m,)), dma((m,)),
            dma((m,)), dma((m,)),
            dma((4,)), dma((4,)),
            dma((4,)), dma((4,)),
        ],
        compiler_params=pltpu.CompilerParams(
            collective_id=0, has_side_effects=True, vmem_limit_bytes=60 << 20
        ),
        name="lent_attention",
    )(query, fresh_key_value, kv_pool, lengths, slot_owner, slot_block)
    out = jnp.transpose(out.reshape(req_dev, steps, 16, WIDTH), (1, 0, 2, 3))
    return out.reshape(steps, req_dev, width)


def solution(mesh):
    placed = (
        P(None, "inst", "tp"),
        P(None, "inst", "tp"),
        P("inst", None, "tp"),
        P("inst"),
        P(("inst", "tp")),
        P(("inst", "tp")),
    )
    return jax.shard_map(
        shards, mesh=mesh, in_specs=placed, out_specs=P(None, "inst", "tp"), check_vma=False
    )
```

```python
import math

import jax
import jax.numpy as jnp
from jax import lax
from jax.experimental import pallas as pl
from jax.experimental.pallas import tpu as pltpu
from jax.sharding import PartitionSpec as P

BLOCK = 2048
WIDTH = 128
ROWS = 64
NX, NZ, NC, NY = 4, 16, 2, 4
GROUPS = NX * NC
SLOTS = 4
SCALE = 1.0 / math.sqrt(WIDTH)
LOG2E = math.log2(math.e)
NEG = -1e30
F32 = jnp.float32
BF16 = jnp.bfloat16

PARENT = {3: 0, -3: 0, 1: 0, -1: 0, 6: 3, 2: 3, 4: 3, -6: -3, -2: -3, -4: -3, 8: 6, 7: 6, 5: 6, -7: -6, -5: -6}
CHILDREN = {p: [o for o in PARENT if PARENT[o] == p] for p in (0, *PARENT)}
PLACE = {o: i for i, o in enumerate(PARENT)}
NEAR = (3, -3, 2, -2, 1, -1)
X_PEERS = (1, 3, 2)


def kernel(
    q_in, fresh_in, kv_ref, len_in, owner_in, block_in, out_ref,
    q_raw, q_ref, fresh_ref, len_ref, owner_ref, block_ref,
    kv, kt, qall, rowtab, ivec, tab_s, ivec_s, sel, got0, got1, parts, lses, lrow, wmat, wcol,
    cbuf, clse, rbuf, rlse, mbuf, mlse, tail, tail_lse,
    in_sem, kv_sem, sm_sem, y_ss, y_rs, t_ss, t_rs, w_ss, w_rs, a_ss, a_rs, h_ss, h_rs, s_ss, s_rs,
    p_ss, p_rs, l_ss, l_rs, u_ss, u_rs, v_ss, v_rs, c_ss, c_rs, d_ss, d_rs,
):
    me = lax.axis_index("inst")
    y = lax.axis_index("tp")
    x, z, c = me // (NZ * NC), (me // NC) % NZ, me % NC
    g = x * NC + c

    def at(dx, dz, dc, dy):
        xx, zz = (x + dx + NX) % NX, (z + dz + NZ) % NZ
        cc, yy = (c + dc) % NC, (y + dy) % NY
        return ((xx * NZ + zz) * NC + cc, yy)

    def send(src, dst, ss, rs, to):
        return pltpu.make_async_remote_copy(
            src_ref=src, dst_ref=dst, send_sem=ss, recv_sem=rs,
            device_id=to, device_id_type=pl.DeviceIdType.MESH,
        )

    peers = [at(0, d, 0, 0) for d in NEAR]
    peers += [at(dx, 0, 0, 0) for dx in X_PEERS] + [at(0, 0, 1, 0)]
    peers += [at(0, 0, 0, d) for d in range(1, NY)]
    barrier = pltpu.get_barrier_semaphore()
    for p in peers:
        pl.semaphore_signal(barrier, inc=1, device_id=p, device_id_type=pl.DeviceIdType.MESH)
    inputs = [
        pltpu.make_async_copy(a, b, in_sem.at[i])
        for i, (a, b) in enumerate(
            ((q_in, q_raw), (len_in, len_ref), (owner_in, owner_ref), (block_in, block_ref), (fresh_in, fresh_ref))
        )
    ]
    for copy in inputs:
        copy.start()
    kv_copies = [pltpu.make_async_copy(kv_ref.at[s], kv.at[s], kv_sem.at[s]) for s in range(SLOTS)]
    for copy in kv_copies:
        copy.start()
    for copy in inputs:
        copy.wait()
    for a in range(4):
        qa = q_raw[a].astype(F32)
        for r in range(2):
            tile = jnp.concatenate([qa[r : r + 1, WIDTH * h : WIDTH * (h + 1)] for h in range(16)], axis=0)
            q_ref[4 * r + a] = tile.astype(BF16)
    row = lax.broadcasted_iota(jnp.int32, (16, WIDTH), 0) % 4
    hi = jnp.where(row < 2, len_ref[0] // 64, len_ref[1] // 64)
    lo = jnp.where(row < 2, len_ref[0] % 64, len_ref[1] % 64)
    qall[z, c, 0:8] = q_ref[...]
    qall[z, c, 8] = jnp.where(row % 2 == 0, hi, lo).astype(F32).astype(BF16)
    rowtab[g, y] = jnp.full((1, WIDTH), owner_ref[0] * 4 + block_ref[0], jnp.int32)
    pl.semaphore_wait(barrier, len(peers))

    sent = []
    spread, hand = {}, []

    def pass_on(o):
        came = qall.at[(z - o + NZ) % NZ, c]
        for k in CHILDREN[o]:
            i = PLACE[k]
            spread[k] = send(came, came, a_ss.at[i], a_rs.at[i], at(0, k - o, 0, 0))
            spread[k].start()
        i = PLACE.get(o, len(PLACE))
        hand.append(send(came, came, h_ss.at[i], h_rs.at[i], at(0, 0, 1, 0)))
        hand[-1].start()

    def arrive(*places):
        for o in places:
            spread[o].wait_recv()
            pass_on(o)

    pass_on(0)
    tables = []
    for i in range(NY - 1):
        tables.append(send(rowtab.at[g, y], rowtab.at[g, y], y_ss.at[i], y_rs.at[i], at(0, 0, 0, i + 1)))
        tables[-1].start()
    for t in tables:
        t.wait_recv()
    along_x, across = [], []
    for i, dx in enumerate(X_PEERS):
        along_x.append(send(rowtab.at[g], rowtab.at[g], t_ss.at[i], t_rs.at[i], at(dx, 0, 0, 0)))
        along_x[-1].start()

    def table_to_sibling(i, gg):
        across.append(send(rowtab.at[gg], rowtab.at[gg], w_ss.at[i], w_rs.at[i], at(0, 0, 1, 0)))
        across[-1].start()

    table_to_sibling(3, g)

    for r in range(2):
        qf = q_ref[4 * r : 4 * r + 4].reshape(ROWS, WIDTH).astype(F32)
        step = lax.broadcasted_iota(jnp.int32, (ROWS, 1), 0) // 16
        ss = []
        for b in range(4):
            k_b = fresh_ref[b].astype(F32)[r : r + 1, :WIDTH]
            s_b = jnp.sum(qf * k_b, axis=1, keepdims=True) * SCALE
            ss.append(jnp.where(step >= b, s_b, -jnp.inf))
        top = jnp.maximum(jnp.maximum(ss[0], ss[1]), jnp.maximum(ss[2], ss[3]))
        ws = [jnp.exp(s_b - top) for s_b in ss]
        total = ws[0] + ws[1] + ws[2] + ws[3]
        acc = jnp.zeros((ROWS, WIDTH), F32)
        for b in range(4):
            v_b = fresh_ref[b].astype(F32)[r : r + 1, WIDTH:]
            acc = acc + ws[b].astype(BF16).astype(F32) * v_b
        tail[r] = acc / total
        tail_lse[r] = jnp.broadcast_to(top + jnp.log(total), (ROWS, WIDTH))

    arrive(1, -1, 3, -3)

    for s in range(SLOTS):
        kv_copies[s].wait()
        kt[s] = kv[s, :, :WIDTH].T

    for i, dx in enumerate(X_PEERS):
        along_x[i].wait_recv()
        table_to_sibling(i, ((x - dx + NX) % NX) * NC + c)
    arrive(2, 4, -2, -4, 6, -6)

    for t in across:
        t.wait_recv()
    lane = lax.broadcasted_iota(jnp.int32, (1, WIDTH), 1)
    want = (((x * NZ + (lane % 32) // 2) * NC + c) * 2 + lane % 2) * 4 + lane // 32
    index = jnp.zeros((1, WIDTH), jnp.int32)
    count = jnp.zeros((1, WIDTH), jnp.int32)
    for gg in range(GROUPS):
        for s in range(SLOTS):
            hit = rowtab[gg, s] == want
            index = jnp.where(hit, gg * SLOTS + s, index)
            count = jnp.where(hit, 1, count)
    ivec[0] = index
    ivec[1] = count
    to_smem = [
        pltpu.make_async_copy(rowtab, tab_s, sm_sem.at[0]),
        pltpu.make_async_copy(ivec, ivec_s, sm_sem.at[1]),
    ]
    for copy in to_smem:
        copy.start()
    for copy in to_smem:
        copy.wait()

    arrive(5, 7, -5, -7, 8)
    for t in hand:
        t.wait_recv()

    group = lax.broadcasted_iota(jnp.int32, (16, WIDTH), 0) // 4
    got = (got0, got1)

    def choose(gg, half, ref):
        lens = jnp.zeros((16, WIDTH), F32)
        for i in range(2):
            owner = tab_s[gg, 2 * half + i, 0, 0] // 4
            zz, cc, r = (owner // 4) % NZ, (owner // 2) % NC, owner % 2
            ref[4 * i : 4 * i + 4] = qall[zz, cc, pl.ds(4 * r, 4)]
            lens = jnp.where(group == i, qall[zz, cc, 8].astype(F32), lens)
        ref[8] = lens.astype(BF16)

    queries = []
    for half in range(2):
        for i, dx in enumerate(X_PEERS):
            choose(((x + dx) % NX) * NC + c, half, sel.at[i, half])
            copy = send(
                sel.at[i, half], got[half].at[x], s_ss.at[i, half], s_rs.at[i, half], at(dx, 0, 0, 0)
            )
            copy.start()
            queries.append(copy)
        choose(g, half, got[half].at[x])

    lane_pos = lax.broadcasted_iota(jnp.int32, (1, BLOCK), 1).astype(F32)
    lane_id = lax.broadcasted_iota(jnp.int32, (ROWS, WIDTH), 1)
    lcols = jnp.zeros((ROWS, WIDTH), F32)
    back = []
    for half in range(2):
        for t in queries[half * len(X_PEERS) : (half + 1) * len(X_PEERS)]:
            t.wait_recv()
        for n in range(2):
            s = 2 * half + n
            code = tab_s[g, s, 0, 0]
            owner, blk = code // 4, code % 4
            src = owner // 64
            r = owner % 2
            q = got[half][src, 4 * n : 4 * n + 4].reshape(ROWS, WIDTH)
            lens = got[half][src, 8].astype(F32)
            hi = jnp.where(r == 0, lens[4 * n : 4 * n + 1], lens[4 * n + 2 : 4 * n + 3])
            lo = jnp.where(r == 0, lens[4 * n + 1 : 4 * n + 2], lens[4 * n + 3 : 4 * n + 4])
            left = (hi * 64.0 + lo)[:, :1] - (blk * BLOCK).astype(F32)
            scores = jnp.dot(q, kt[s], preferred_element_type=F32)
            scores = jnp.where(lane_pos < left, scores, -jnp.inf)
            top = jnp.max(scores, axis=1, keepdims=True)
            weights = jnp.exp2((scores - top) * (SCALE * LOG2E))
            total = jnp.sum(weights, axis=1, keepdims=True)
            part = jnp.dot(weights.astype(BF16), kv[s, :, WIDTH:], preferred_element_type=F32) / total
            parts[g, s] = part.astype(BF16).reshape(4, 16, WIDTH)
            lcols = jnp.where(lane_id == s, top * SCALE + jnp.log(total), lcols)
        mine = parts.at[g, 2 * half : 2 * half + 2]
        for i in range(4):
            to = at(X_PEERS[i], 0, 0, 0) if i < 3 else at(0, 0, 1, 0)
            copy = send(mine, mine, p_ss.at[i, half], p_rs.at[i, half], to)
            copy.start()
            back.append(copy)
    lt = jnp.concatenate([lcols, lcols], axis=0).T
    for s in range(SLOTS):
        lses[g, s] = lt[s : s + 1]
    lse_sent = []
    for i in range(4):
        to = at(X_PEERS[i], 0, 0, 0) if i < 3 else at(0, 0, 1, 0)
        copy = send(lses.at[g], lses.at[g], l_ss.at[i], l_rs.at[i], to)
        copy.start()
        lse_sent.append(copy)
    handed = []
    for half in range(2):
        for i, dx in enumerate(X_PEERS):
            back[half * 4 + i].wait_recv()
            there = parts.at[((x - dx + NX) % NX) * NC + c, 2 * half : 2 * half + 2]
            copy = send(there, there, u_ss.at[i, half], u_rs.at[i, half], at(0, 0, 1, 0))
            copy.start()
            handed.append(copy)
    for i, dx in enumerate(X_PEERS):
        lse_sent[i].wait_recv()
        there = lses.at[((x - dx + NX) % NX) * NC + c]
        copy = send(there, there, v_ss.at[i], v_rs.at[i], at(0, 0, 1, 0))
        copy.start()
        handed.append(copy)
    for half in range(2):
        back[half * 4 + 3].wait_recv()
    lse_sent[3].wait_recv()
    for copy in handed:
        copy.wait_recv()
    back = back + lse_sent + handed

    half = lax.broadcasted_iota(jnp.int32, (1, WIDTH), 1) < ROWS
    wmat[...] = jnp.zeros((WIDTH, WIDTH), F32)

    def where_is(d, r, k):
        j = k * 32 + ((z + d) % NZ) * 2 + r
        return ivec_s[0, 0, j], ivec_s[1, 0, j]

    for d in range(NZ):
        for k in range(3):
            pair = []
            for r in range(2):
                i, n = where_is(d, r, k)
                pair.append(jnp.where(n > 0, lses[i // 4, i % 4], NEG))
            lrow[k, d] = jnp.where(half, pair[0], pair[1])[0]
    l0, l1, l2 = lrow[0], lrow[1], lrow[2]
    peak = jnp.maximum(jnp.maximum(l0, l1), l2)
    w0, w1, w2 = jnp.exp(l0 - peak), jnp.exp(l1 - peak), jnp.exp(l2 - peak)
    total = w0 + w1 + w2
    merged = peak + jnp.log(total)
    wmat[0:16] = w0 / total
    wmat[16:32] = w1 / total
    wmat[32:48] = w2 / total
    for d in range(NZ):
        clse[d] = merged[d : d + 1]
    wcol[...] = wmat[...].T

    def build(d):
        d = d % NZ
        for r in range(2):
            acc = jnp.zeros((ROWS, WIDTH), F32)
            for k in range(3):
                i, _ = where_is(d, r, k)
                p = parts[i // 4, i % 4].reshape(ROWS, WIDTH).astype(F32)
                acc = acc + wcol[r * ROWS : (r + 1) * ROWS, k * 16 + d : k * 16 + d + 1] * p
            cbuf[d, 4 * r : 4 * r + 4] = acc.astype(BF16).reshape(4, 16, WIDTH)

    up = {}

    def send_up(o, data, lse):
        i = PLACE[o]
        to = at(0, PARENT[o] - o, 0, 0)
        up[o] = (
            send(data, rbuf.at[i], c_ss.at[i], c_rs.at[i], to),
            send(lse, rlse.at[i], d_ss.at[i], d_rs.at[i], to),
        )
        for copy in up[o]:
            copy.start()

    def gather_up(o):
        for k in CHILDREN[o]:
            for copy in up[k]:
                copy.wait_recv()

    for o in (5, 7, 8, -5, -7, 2, 4, -2, -4, 1, -1):
        build(-o)
        send_up(o, cbuf.at[-o % NZ], clse.at[-o % NZ])
    for o in (6, -6, 3, -3, 0):
        build(-o)
    for n, o in enumerate((6, -6, 3, -3)):
        gather_up(o)
        ls = [clse[-o % NZ]] + [rlse[PLACE[k]] for k in CHILDREN[o]]
        data = [cbuf[-o % NZ]] + [rbuf[PLACE[k]] for k in CHILDREN[o]]
        peak = ls[0]
        for l in ls[1:]:
            peak = jnp.maximum(peak, l)
        ws = [jnp.exp(l - peak) for l in ls]
        total = ws[0]
        for w in ws[1:]:
            total = total + w
        mlse[n] = peak + jnp.log(total)
        for i, w in enumerate(ws):
            wmat[i : i + 1] = w / total
        wt = wmat[...].T
        acc = jnp.zeros((WIDTH, WIDTH), F32)
        for i, p in enumerate(data):
            acc = acc + wt[:, i : i + 1] * p.reshape(WIDTH, WIDTH).astype(F32)
        mbuf[n] = acc.astype(BF16).reshape(8, 16, WIDTH)
        send_up(o, mbuf.at[n], mlse.at[n])
    gather_up(0)
    for i, k in enumerate(CHILDREN[0]):
        wmat[i : i + 1] = rlse[PLACE[k]]
    wmat[4:5] = clse[0]
    wt = wmat[...].T
    done = []
    for r in range(2):
        rs = slice(r * ROWS, (r + 1) * ROWS)
        tl = tail_lse[r][:, :1]
        ls = [wt[rs, n : n + 1] for n in range(5)]
        peak = tl
        for l in ls:
            peak = jnp.maximum(peak, l)
        w = jnp.exp(tl - peak)
        denom = w
        acc = w * tail[r]
        for n, ref in enumerate([rbuf.at[PLACE[k]] for k in CHILDREN[0]] + [cbuf.at[0]]):
            w = jnp.exp(ls[n] - peak)
            denom = denom + w
            acc = acc + w * ref[4 * r : 4 * r + 4].reshape(ROWS, WIDTH).astype(F32)
        done.append(acc / denom)
    for a in range(4):
        heads = [
            jnp.concatenate([done[0][i : i + 1], done[1][i : i + 1]], axis=0)
            for i in range(16 * a, 16 * a + 16)
        ]
        out_ref[a] = jnp.concatenate(heads, axis=1).astype(BF16)

    for copy in [*spread.values(), *hand, *tables, *along_x, *across, *queries, *back]:
        copy.wait_send()
    for pair in up.values():
        for copy in pair:
            copy.wait_send()


def shards(query, fresh_key_value, kv_pool, lengths, slot_owner, slot_block):
    dma = pltpu.SemaphoreType.DMA
    hbm = pl.BlockSpec(memory_space=pl.ANY)
    m = len(PARENT)
    return pl.pallas_call(
        kernel,
        out_shape=jax.ShapeDtypeStruct(query.shape, BF16),
        in_specs=[hbm] * 6,
        out_specs=pl.BlockSpec(memory_space=pltpu.VMEM),
        scratch_shapes=[
            pltpu.VMEM(query.shape, BF16),
            pltpu.VMEM((8, 16, WIDTH), BF16),
            pltpu.VMEM(fresh_key_value.shape, BF16),
            pltpu.SMEM(lengths.shape, jnp.int32),
            pltpu.SMEM(slot_owner.shape, jnp.int32),
            pltpu.SMEM(slot_block.shape, jnp.int32),
            pltpu.VMEM((SLOTS, BLOCK, 2 * WIDTH), BF16),
            pltpu.VMEM((SLOTS, WIDTH, BLOCK), BF16),
            pltpu.VMEM((NZ, NC, 9, 16, WIDTH), BF16),
            pltpu.VMEM((GROUPS, SLOTS, 1, WIDTH), jnp.int32),
            pltpu.VMEM((2, 1, WIDTH), jnp.int32),
            pltpu.SMEM((GROUPS, SLOTS, 1, WIDTH), jnp.int32),
            pltpu.SMEM((2, 1, WIDTH), jnp.int32),
            pltpu.VMEM((3, 2, 9, 16, WIDTH), BF16),
            pltpu.VMEM((NX, 9, 16, WIDTH), BF16),
            pltpu.VMEM((NX, 9, 16, WIDTH), BF16),
            pltpu.VMEM((GROUPS, SLOTS, 4, 16, WIDTH), BF16),
            pltpu.VMEM((GROUPS, SLOTS, 1, WIDTH), F32),
            pltpu.VMEM((3, NZ, WIDTH), F32),
            pltpu.VMEM((WIDTH, WIDTH), F32),
            pltpu.VMEM((WIDTH, WIDTH), F32),
            pltpu.VMEM((NZ, 8, 16, WIDTH), BF16),
            pltpu.VMEM((NZ, 1, WIDTH), F32),
            pltpu.VMEM((m, 8, 16, WIDTH), BF16),
            pltpu.VMEM((m, 1, WIDTH), F32),
            pltpu.VMEM((4, 8, 16, WIDTH), BF16),
            pltpu.VMEM((4, 1, WIDTH), F32),
            pltpu.VMEM((2, ROWS, WIDTH), F32),
            pltpu.VMEM((2, ROWS, WIDTH), F32),
            dma((5,)),
            dma((SLOTS,)),
            dma((2,)),
            dma((3,)), dma((3,)),
            dma((3,)), dma((3,)),
            dma((4,)), dma((4,)),
            dma((m,)), dma((m,)),
            dma((m + 1,)), dma((m + 1,)),
            dma((3, 2)), dma((3, 2)),
            dma((4, 2)), dma((4, 2)),
            dma((4,)), dma((4,)),
            dma((3, 2)), dma((3, 2)),
            dma((3,)), dma((3,)),
            dma((m,)), dma((m,)),
            dma((m,)), dma((m,)),
        ],
        compiler_params=pltpu.CompilerParams(
            collective_id=0, has_side_effects=True, vmem_limit_bytes=60 << 20
        ),
        name="lent_attention",
    )(query, fresh_key_value, kv_pool, lengths, slot_owner, slot_block)


def solution(mesh):
    placed = (
        P(None, "inst", "tp"),
        P(None, "inst", "tp"),
        P("inst", None, "tp"),
        P("inst"),
        P(("inst", "tp")),
        P(("inst", "tp")),
    )
    return jax.shard_map(
        shards, mesh=mesh, in_specs=placed, out_specs=P(None, "inst", "tp"), check_vma=False
    )
```

```python
import math

import jax
import jax.numpy as jnp
from jax import lax
from jax.experimental import pallas as pl
from jax.experimental.pallas import tpu as pltpu
from jax.sharding import PartitionSpec as P

BLOCK = 2048
WIDTH = 128
ROWS = 64
NX, NZ, NC, NY = 4, 16, 2, 4
GROUPS = NX * NC
SLOTS = 4
SCALE = 1.0 / math.sqrt(WIDTH)
LOG2E = math.log2(math.e)
NEG = -1e30
F32 = jnp.float32
BF16 = jnp.bfloat16

PARENT = {3: 0, -3: 0, 1: 0, -1: 0, 6: 3, 2: 3, 4: 3, -6: -3, -2: -3, -4: -3, 8: 6, 7: 6, 5: 6, -7: -6, -5: -6}
CHILDREN = {p: [o for o in PARENT if PARENT[o] == p] for p in (0, *PARENT)}
PLACE = {o: i for i, o in enumerate(PARENT)}
NEAR = (3, -3, 2, -2, 1, -1)
X_PEERS = (2, 1, 3)


def kernel(
    q_in, fresh_in, kv_ref, len_in, owner_in, block_in, out_ref,
    q_raw, q_ref, fresh_ref, len_ref, owner_ref, block_ref,
    kv, kt, qall, rowtab, ivec, tab_s, ivec_s, sel, got0, got1, parts, lses, lrow, wmat, wcol,
    cbuf, clse, rbuf, rlse, mbuf, mlse, tail, tail_lse,
    in_sem, kv_sem, sm_sem, y_ss, y_rs, t_ss, t_rs, w_ss, w_rs, a_ss, a_rs, h_ss, h_rs, s_ss, s_rs,
    p_ss, p_rs, l_ss, l_rs, u_ss, u_rs, v_ss, v_rs, c_ss, c_rs, d_ss, d_rs,
):
    me = lax.axis_index("inst")
    y = lax.axis_index("tp")
    x, z, c = me // (NZ * NC), (me // NC) % NZ, me % NC
    g = x * NC + c

    def at(dx, dz, dc, dy):
        xx, zz = (x + dx + NX) % NX, (z + dz + NZ) % NZ
        cc, yy = (c + dc) % NC, (y + dy) % NY
        return ((xx * NZ + zz) * NC + cc, yy)

    def send(src, dst, ss, rs, to):
        return pltpu.make_async_remote_copy(
            src_ref=src, dst_ref=dst, send_sem=ss, recv_sem=rs,
            device_id=to, device_id_type=pl.DeviceIdType.MESH,
        )

    peers = [at(0, d, 0, 0) for d in NEAR]
    peers += [at(dx, 0, 0, 0) for dx in X_PEERS] + [at(0, 0, 1, 0)]
    peers += [at(0, 0, 0, d) for d in range(1, NY)]
    barrier = pltpu.get_barrier_semaphore()
    for p in peers:
        pl.semaphore_signal(barrier, inc=1, device_id=p, device_id_type=pl.DeviceIdType.MESH)
    inputs = [
        pltpu.make_async_copy(a, b, in_sem.at[i])
        for i, (a, b) in enumerate(
            ((q_in, q_raw), (len_in, len_ref), (owner_in, owner_ref), (block_in, block_ref), (fresh_in, fresh_ref))
        )
    ]
    for copy in inputs:
        copy.start()
    kv_copies = [pltpu.make_async_copy(kv_ref.at[s], kv.at[s], kv_sem.at[s]) for s in range(SLOTS)]
    for copy in kv_copies:
        copy.start()
    for copy in inputs:
        copy.wait()
    for a in range(4):
        qa = q_raw[a].astype(F32)
        for r in range(2):
            tile = jnp.concatenate([qa[r : r + 1, WIDTH * h : WIDTH * (h + 1)] for h in range(16)], axis=0)
            q_ref[4 * r + a] = tile.astype(BF16)
    row = lax.broadcasted_iota(jnp.int32, (16, WIDTH), 0) % 4
    hi = jnp.where(row < 2, len_ref[0] // 64, len_ref[1] // 64)
    lo = jnp.where(row < 2, len_ref[0] % 64, len_ref[1] % 64)
    qall[z, c, 0:8] = q_ref[...]
    qall[z, c, 8] = jnp.where(row % 2 == 0, hi, lo).astype(F32).astype(BF16)
    rowtab[g, y] = jnp.full((1, WIDTH), owner_ref[0] * 4 + block_ref[0], jnp.int32)
    pl.semaphore_wait(barrier, len(peers))

    sent = []
    spread, hand = {}, []

    def pass_on(o):
        came = qall.at[(z - o + NZ) % NZ, c]
        for k in CHILDREN[o]:
            i = PLACE[k]
            spread[k] = send(came, came, a_ss.at[i], a_rs.at[i], at(0, k - o, 0, 0))
            spread[k].start()
        i = PLACE.get(o, len(PLACE))
        hand.append(send(came, came, h_ss.at[i], h_rs.at[i], at(0, 0, 1, 0)))
        hand[-1].start()

    def arrive(*places):
        for o in places:
            spread[o].wait_recv()
            pass_on(o)

    pass_on(0)
    tables = []
    for i in range(NY - 1):
        tables.append(send(rowtab.at[g, y], rowtab.at[g, y], y_ss.at[i], y_rs.at[i], at(0, 0, 0, i + 1)))
        tables[-1].start()
    for t in tables:
        t.wait_recv()
    along_x, across = [], []
    for i, dx in enumerate(X_PEERS):
        along_x.append(send(rowtab.at[g], rowtab.at[g], t_ss.at[i], t_rs.at[i], at(dx, 0, 0, 0)))
        along_x[-1].start()

    def table_to_sibling(i, gg):
        across.append(send(rowtab.at[gg], rowtab.at[gg], w_ss.at[i], w_rs.at[i], at(0, 0, 1, 0)))
        across[-1].start()

    table_to_sibling(3, g)

    for r in range(2):
        qf = q_ref[4 * r : 4 * r + 4].reshape(ROWS, WIDTH).astype(F32)
        step = lax.broadcasted_iota(jnp.int32, (ROWS, 1), 0) // 16
        ss = []
        for b in range(4):
            k_b = fresh_ref[b].astype(F32)[r : r + 1, :WIDTH]
            s_b = jnp.sum(qf * k_b, axis=1, keepdims=True) * SCALE
            ss.append(jnp.where(step >= b, s_b, -jnp.inf))
        top = jnp.maximum(jnp.maximum(ss[0], ss[1]), jnp.maximum(ss[2], ss[3]))
        ws = [jnp.exp(s_b - top) for s_b in ss]
        total = ws[0] + ws[1] + ws[2] + ws[3]
        acc = jnp.zeros((ROWS, WIDTH), F32)
        for b in range(4):
            v_b = fresh_ref[b].astype(F32)[r : r + 1, WIDTH:]
            acc = acc + ws[b].astype(BF16).astype(F32) * v_b
        tail[r] = acc / total
        tail_lse[r] = jnp.broadcast_to(top + jnp.log(total), (ROWS, WIDTH))

    arrive(1, -1, 3, -3)

    for s in range(SLOTS):
        kv_copies[s].wait()
        kt[s] = kv[s, :, :WIDTH].T

    for i, dx in enumerate(X_PEERS):
        along_x[i].wait_recv()
        table_to_sibling(i, ((x - dx + NX) % NX) * NC + c)
    arrive(2, 4, -2, -4, 6, -6)

    for t in across:
        t.wait_recv()
    lane = lax.broadcasted_iota(jnp.int32, (1, WIDTH), 1)
    want = (((x * NZ + (lane % 32) // 2) * NC + c) * 2 + lane % 2) * 4 + lane // 32
    index = jnp.zeros((1, WIDTH), jnp.int32)
    count = jnp.zeros((1, WIDTH), jnp.int32)
    for gg in range(GROUPS):
        for s in range(SLOTS):
            hit = rowtab[gg, s] == want
            index = jnp.where(hit, gg * SLOTS + s, index)
            count = jnp.where(hit, 1, count)
    ivec[0] = index
    ivec[1] = count
    to_smem = [
        pltpu.make_async_copy(rowtab, tab_s, sm_sem.at[0]),
        pltpu.make_async_copy(ivec, ivec_s, sm_sem.at[1]),
    ]
    for copy in to_smem:
        copy.start()
    for copy in to_smem:
        copy.wait()

    arrive(5, 7, -5, -7, 8)
    for t in hand:
        t.wait_recv()

    group = lax.broadcasted_iota(jnp.int32, (16, WIDTH), 0) // 4
    got = (got0, got1)

    def choose(gg, half, ref):
        lens = jnp.zeros((16, WIDTH), F32)
        for i in range(2):
            owner = tab_s[gg, 2 * half + i, 0, 0] // 4
            zz, cc, r = (owner // 4) % NZ, (owner // 2) % NC, owner % 2
            ref[4 * i : 4 * i + 4] = qall[zz, cc, pl.ds(4 * r, 4)]
            lens = jnp.where(group == i, qall[zz, cc, 8].astype(F32), lens)
        ref[8] = lens.astype(BF16)

    queries = []
    for half in range(2):
        for i, dx in enumerate(X_PEERS):
            choose(((x + dx) % NX) * NC + c, half, sel.at[i, half])
            copy = send(
                sel.at[i, half], got[half].at[x], s_ss.at[i, half], s_rs.at[i, half], at(dx, 0, 0, 0)
            )
            copy.start()
            queries.append(copy)
        choose(g, half, got[half].at[x])

    lane_pos = lax.broadcasted_iota(jnp.int32, (1, BLOCK), 1).astype(F32)
    lane_id = lax.broadcasted_iota(jnp.int32, (ROWS, WIDTH), 1)
    lcols = jnp.zeros((ROWS, WIDTH), F32)
    back, lse_sent = [], []
    for half in range(2):
        for t in queries[half * len(X_PEERS) : (half + 1) * len(X_PEERS)]:
            t.wait_recv()
        rounded, totals = [], []
        for n in range(2):
            s = 2 * half + n
            code = tab_s[g, s, 0, 0]
            owner, blk = code // 4, code % 4
            src = owner // 64
            r = owner % 2
            q = got[half][src, 4 * n : 4 * n + 4].reshape(ROWS, WIDTH)
            lens = got[half][src, 8].astype(F32)
            hi = jnp.where(r == 0, lens[4 * n : 4 * n + 1], lens[4 * n + 2 : 4 * n + 3])
            lo = jnp.where(r == 0, lens[4 * n + 1 : 4 * n + 2], lens[4 * n + 3 : 4 * n + 4])
            left = (hi * 64.0 + lo)[:, :1] - (blk * BLOCK).astype(F32)
            scores = jnp.dot(q, kt[s], preferred_element_type=F32)
            scores = jnp.where(lane_pos < left, scores, -jnp.inf)
            top = jnp.max(scores, axis=1, keepdims=True)
            weights = jnp.exp2((scores - top) * (SCALE * LOG2E))
            total = jnp.sum(weights, axis=1, keepdims=True)
            lcols = jnp.where(lane_id == s, top * SCALE + jnp.log(total), lcols)
            rounded.append(weights.astype(BF16))
            totals.append(total)
        if half == 1:
            lt = jnp.concatenate([lcols, lcols], axis=0).T
            for s in range(SLOTS):
                lses[g, s] = lt[s : s + 1]
            for i in range(4):
                to = at(X_PEERS[i], 0, 0, 0) if i < 3 else at(0, 0, 1, 0)
                copy = send(lses.at[g], lses.at[g], l_ss.at[i], l_rs.at[i], to)
                copy.start()
                lse_sent.append(copy)
        for n in range(2):
            s = 2 * half + n
            part = jnp.dot(rounded[n], kv[s, :, WIDTH:], preferred_element_type=F32) / totals[n]
            parts[g, s] = part.astype(BF16).reshape(4, 16, WIDTH)
        mine = parts.at[g, 2 * half : 2 * half + 2]
        for i in range(4):
            to = at(X_PEERS[i], 0, 0, 0) if i < 3 else at(0, 0, 1, 0)
            copy = send(mine, mine, p_ss.at[i, half], p_rs.at[i, half], to)
            copy.start()
            back.append(copy)
    for copy in [*spread.values(), *hand, *tables, *along_x, *across, *queries]:
        copy.wait_send()

    handed = []

    def hand_parts(half):
        for i, dx in enumerate(X_PEERS):
            back[half * 4 + i].wait_recv()
            there = parts.at[((x - dx + NX) % NX) * NC + c, 2 * half : 2 * half + 2]
            copy = send(there, there, u_ss.at[i, half], u_rs.at[i, half], at(0, 0, 1, 0))
            copy.start()
            handed.append(copy)

    hand_parts(0)
    lse_handed = []
    for i, dx in enumerate(X_PEERS):
        lse_sent[i].wait_recv()
        there = lses.at[((x - dx + NX) % NX) * NC + c]
        copy = send(there, there, v_ss.at[i], v_rs.at[i], at(0, 0, 1, 0))
        copy.start()
        lse_handed.append(copy)
    hand_parts(1)
    lse_sent[3].wait_recv()
    for copy in lse_handed:
        copy.wait_recv()

    half = lax.broadcasted_iota(jnp.int32, (1, WIDTH), 1) < ROWS
    wmat[...] = jnp.zeros((WIDTH, WIDTH), F32)

    def where_is(d, r, k):
        j = k * 32 + ((z + d) % NZ) * 2 + r
        return ivec_s[0, 0, j], ivec_s[1, 0, j]

    for d in range(NZ):
        for k in range(3):
            pair = []
            for r in range(2):
                i, n = where_is(d, r, k)
                pair.append(jnp.where(n > 0, lses[i // 4, i % 4], NEG))
            lrow[k, d] = jnp.where(half, pair[0], pair[1])[0]
    l0, l1, l2 = lrow[0], lrow[1], lrow[2]
    peak = jnp.maximum(jnp.maximum(l0, l1), l2)
    w0, w1, w2 = jnp.exp(l0 - peak), jnp.exp(l1 - peak), jnp.exp(l2 - peak)
    total = w0 + w1 + w2
    merged = peak + jnp.log(total)
    wmat[0:16] = w0 / total
    wmat[16:32] = w1 / total
    wmat[32:48] = w2 / total
    for d in range(NZ):
        clse[d] = merged[d : d + 1]
    wcol[...] = wmat[...].T

    def build(d):
        d = d % NZ
        for r in range(2):
            acc = jnp.zeros((ROWS, WIDTH), F32)
            for k in range(3):
                i, _ = where_is(d, r, k)
                p = parts[i // 4, i % 4].reshape(ROWS, WIDTH).astype(F32)
                acc = acc + wcol[r * ROWS : (r + 1) * ROWS, k * 16 + d : k * 16 + d + 1] * p
            cbuf[d, 4 * r : 4 * r + 4] = acc.astype(BF16).reshape(4, 16, WIDTH)

    for half in range(2):
        back[half * 4 + 3].wait_recv()
    for copy in handed:
        copy.wait_recv()

    up = {}

    def send_up(o, data, lse):
        i = PLACE[o]
        to = at(0, PARENT[o] - o, 0, 0)
        up[o] = (
            send(data, rbuf.at[i], c_ss.at[i], c_rs.at[i], to),
            send(lse, rlse.at[i], d_ss.at[i], d_rs.at[i], to),
        )
        for copy in up[o]:
            copy.start()

    def gather_up(o):
        for k in CHILDREN[o]:
            for copy in up[k]:
                copy.wait_recv()

    for o in (5, 7, 8, -5, -7, 2, 4, -2, -4, 1, -1):
        build(-o)
        send_up(o, cbuf.at[-o % NZ], clse.at[-o % NZ])
    for o in (6, -6, 3, -3, 0):
        build(-o)
    for copy in [*back, *lse_sent, *handed, *lse_handed]:
        copy.wait_send()
    for n, o in enumerate((6, -6, 3, -3)):
        gather_up(o)
        ls = [clse[-o % NZ]] + [rlse[PLACE[k]] for k in CHILDREN[o]]
        data = [cbuf[-o % NZ]] + [rbuf[PLACE[k]] for k in CHILDREN[o]]
        peak = ls[0]
        for l in ls[1:]:
            peak = jnp.maximum(peak, l)
        ws = [jnp.exp(l - peak) for l in ls]
        total = ws[0]
        for w in ws[1:]:
            total = total + w
        mlse[n] = peak + jnp.log(total)
        for i, w in enumerate(ws):
            wmat[i : i + 1] = w / total
        wt = wmat[0:8].T
        acc = jnp.zeros((WIDTH, WIDTH), F32)
        for i, p in enumerate(data):
            acc = acc + wt[:, i : i + 1] * p.reshape(WIDTH, WIDTH).astype(F32)
        mbuf[n] = acc.astype(BF16).reshape(8, 16, WIDTH)
        send_up(o, mbuf.at[n], mlse.at[n])
    for o in up:
        if o not in (3, -3):
            for copy in up[o]:
                copy.wait_send()
    gather_up(0)
    for i, k in enumerate(CHILDREN[0]):
        wmat[i : i + 1] = rlse[PLACE[k]]
    wmat[4:5] = clse[0]
    wt = wmat[0:8].T
    done = []
    for r in range(2):
        rs = slice(r * ROWS, (r + 1) * ROWS)
        tl = tail_lse[r][:, :1]
        ls = [wt[rs, n : n + 1] for n in range(5)]
        peak = tl
        for l in ls:
            peak = jnp.maximum(peak, l)
        w = jnp.exp(tl - peak)
        denom = w
        acc = w * tail[r]
        for n, ref in enumerate([rbuf.at[PLACE[k]] for k in CHILDREN[0]] + [cbuf.at[0]]):
            w = jnp.exp(ls[n] - peak)
            denom = denom + w
            acc = acc + w * ref[4 * r : 4 * r + 4].reshape(ROWS, WIDTH).astype(F32)
        done.append(acc / denom)
    for a in range(4):
        heads = [
            jnp.concatenate([done[0][i : i + 1], done[1][i : i + 1]], axis=0)
            for i in range(16 * a, 16 * a + 16)
        ]
        out_ref[a] = jnp.concatenate(heads, axis=1).astype(BF16)

    for o in (3, -3):
        for copy in up[o]:
            copy.wait_send()


def shards(query, fresh_key_value, kv_pool, lengths, slot_owner, slot_block):
    dma = pltpu.SemaphoreType.DMA
    hbm = pl.BlockSpec(memory_space=pl.ANY)
    m = len(PARENT)
    return pl.pallas_call(
        kernel,
        out_shape=jax.ShapeDtypeStruct(query.shape, BF16),
        in_specs=[hbm] * 6,
        out_specs=pl.BlockSpec(memory_space=pltpu.VMEM),
        scratch_shapes=[
            pltpu.VMEM(query.shape, BF16),
            pltpu.VMEM((8, 16, WIDTH), BF16),
            pltpu.VMEM(fresh_key_value.shape, BF16),
            pltpu.SMEM(lengths.shape, jnp.int32),
            pltpu.SMEM(slot_owner.shape, jnp.int32),
            pltpu.SMEM(slot_block.shape, jnp.int32),
            pltpu.VMEM((SLOTS, BLOCK, 2 * WIDTH), BF16),
            pltpu.VMEM((SLOTS, WIDTH, BLOCK), BF16),
            pltpu.VMEM((NZ, NC, 9, 16, WIDTH), BF16),
            pltpu.VMEM((GROUPS, SLOTS, 1, WIDTH), jnp.int32),
            pltpu.VMEM((2, 1, WIDTH), jnp.int32),
            pltpu.SMEM((GROUPS, SLOTS, 1, WIDTH), jnp.int32),
            pltpu.SMEM((2, 1, WIDTH), jnp.int32),
            pltpu.VMEM((3, 2, 9, 16, WIDTH), BF16),
            pltpu.VMEM((NX, 9, 16, WIDTH), BF16),
            pltpu.VMEM((NX, 9, 16, WIDTH), BF16),
            pltpu.VMEM((GROUPS, SLOTS, 4, 16, WIDTH), BF16),
            pltpu.VMEM((GROUPS, SLOTS, 1, WIDTH), F32),
            pltpu.VMEM((3, NZ, WIDTH), F32),
            pltpu.VMEM((WIDTH, WIDTH), F32),
            pltpu.VMEM((WIDTH, WIDTH), F32),
            pltpu.VMEM((NZ, 8, 16, WIDTH), BF16),
            pltpu.VMEM((NZ, 1, WIDTH), F32),
            pltpu.VMEM((m, 8, 16, WIDTH), BF16),
            pltpu.VMEM((m, 1, WIDTH), F32),
            pltpu.VMEM((4, 8, 16, WIDTH), BF16),
            pltpu.VMEM((4, 1, WIDTH), F32),
            pltpu.VMEM((2, ROWS, WIDTH), F32),
            pltpu.VMEM((2, ROWS, WIDTH), F32),
            dma((5,)),
            dma((SLOTS,)),
            dma((2,)),
            dma((3,)), dma((3,)),
            dma((3,)), dma((3,)),
            dma((4,)), dma((4,)),
            dma((m,)), dma((m,)),
            dma((m + 1,)), dma((m + 1,)),
            dma((3, 2)), dma((3, 2)),
            dma((4, 2)), dma((4, 2)),
            dma((4,)), dma((4,)),
            dma((3, 2)), dma((3, 2)),
            dma((3,)), dma((3,)),
            dma((m,)), dma((m,)),
            dma((m,)), dma((m,)),
        ],
        compiler_params=pltpu.CompilerParams(
            collective_id=0, has_side_effects=True, vmem_limit_bytes=60 << 20
        ),
        name="lent_attention",
    )(query, fresh_key_value, kv_pool, lengths, slot_owner, slot_block)


def solution(mesh):
    placed = (
        P(None, "inst", "tp"),
        P(None, "inst", "tp"),
        P("inst", None, "tp"),
        P("inst"),
        P(("inst", "tp")),
        P(("inst", "tp")),
    )
    return jax.shard_map(
        shards, mesh=mesh, in_specs=placed, out_specs=P(None, "inst", "tp"), check_vma=False
    )
```

```python
import math

import jax
import jax.numpy as jnp
from jax import lax
from jax.experimental import pallas as pl
from jax.experimental.pallas import tpu as pltpu
from jax.sharding import PartitionSpec as P

BLOCK = 2048
WIDTH = 128
ROWS = 64
NX, NZ, NC, NY = 4, 16, 2, 4
GROUPS = NX * NC
SLOTS = 4
SCALE = 1.0 / math.sqrt(WIDTH)
LOG2E = math.log2(math.e)
NEG = -1e30
F32 = jnp.float32
BF16 = jnp.bfloat16

DOWN = {3: 0, -3: 0, 1: 0, -1: 0, 6: 3, 2: 3, 4: 3, -6: -3, -2: -3, -4: -3, 8: 6, 7: 6, 5: 6, -7: -6, -5: -6}
PARENT = {3: 0, -3: 0, 1: 0, -1: 0, 6: 3, 2: 3, 4: 3, -6: -3, -2: -3, -4: -3, 8: 6, 7: 6, 5: 6, -7: -6, -5: -6}


def level(tree, o):
    return 0 if o == 0 else 1 + level(tree, tree[o])


def height(tree, o):
    return max([0] + [1 + height(tree, k) for k in tree if tree[k] == o])


BELOW = {p: [o for o in DOWN if DOWN[o] == p] for p in (0, *DOWN)}
CHILDREN = {p: [o for o in PARENT if PARENT[o] == p] for p in (0, *PARENT)}
PLACE = {o: i for i, o in enumerate(PARENT)}
ARRIVE = {n: sorted((o for o in DOWN if level(DOWN, o) == n), key=lambda o: (-height(DOWN, o), abs(o))) for n in range(1, 5)}
LEAVES = sorted((o for o in PARENT if not CHILDREN[o]), key=lambda o: -level(PARENT, o))
HUBS = sorted((o for o in PARENT if CHILDREN[o]), key=lambda o: height(PARENT, o))
NEAR = sorted({t * (o - tree[o]) for tree in (DOWN, PARENT) for o in tree for t in (1, -1)}, key=lambda d: -abs(d))
X_PEERS = (2, 1, 3)


def kernel(
    q_in, fresh_in, kv_ref, len_in, owner_in, block_in, out_ref,
    q_raw, q_ref, fresh_ref, len_ref, owner_ref, block_ref,
    kv, kt, qall, rowtab, ivec, tab_s, ivec_s, sel, got0, got1, parts, lses, wmat, wcol,
    cbuf, clse, rbuf, rlse, mbuf, mlse, tail, tail_lse,
    in_sem, kv_sem, sm_sem, y_ss, y_rs, t_ss, t_rs, w_ss, w_rs, a_ss, a_rs, h_ss, h_rs, s_ss, s_rs,
    p_ss, p_rs, l_ss, l_rs, u_ss, u_rs, v_ss, v_rs, c_ss, c_rs, d_ss, d_rs,
):
    me = lax.axis_index("inst")
    y = lax.axis_index("tp")
    x, z, c = me // (NZ * NC), (me // NC) % NZ, me % NC
    g = x * NC + c

    def at(dx, dz, dc, dy):
        xx, zz = (x + dx + NX) % NX, (z + dz + NZ) % NZ
        cc, yy = (c + dc) % NC, (y + dy) % NY
        return ((xx * NZ + zz) * NC + cc, yy)

    def send(src, dst, ss, rs, to):
        return pltpu.make_async_remote_copy(
            src_ref=src, dst_ref=dst, send_sem=ss, recv_sem=rs,
            device_id=to, device_id_type=pl.DeviceIdType.MESH,
        )

    peers = [at(0, d, 0, 0) for d in NEAR]
    peers += [at(dx, 0, 0, 0) for dx in X_PEERS] + [at(0, 0, 1, 0)]
    peers += [at(0, 0, 0, d) for d in range(1, NY)]
    barrier = pltpu.get_barrier_semaphore()
    for p in peers:
        pl.semaphore_signal(barrier, inc=1, device_id=p, device_id_type=pl.DeviceIdType.MESH)
    inputs = [
        pltpu.make_async_copy(a, b, in_sem.at[i])
        for i, (a, b) in enumerate(
            ((q_in, q_raw), (len_in, len_ref), (owner_in, owner_ref), (block_in, block_ref), (fresh_in, fresh_ref))
        )
    ]
    for copy in inputs:
        copy.start()
    kv_copies = [pltpu.make_async_copy(kv_ref.at[s], kv.at[s], kv_sem.at[s]) for s in range(SLOTS)]
    for copy in kv_copies:
        copy.start()
    for copy in inputs:
        copy.wait()
    for a in range(4):
        qa = q_raw[a].astype(F32)
        for r in range(2):
            tile = jnp.concatenate([qa[r : r + 1, WIDTH * h : WIDTH * (h + 1)] for h in range(16)], axis=0)
            q_ref[4 * r + a] = tile.astype(BF16)
    row = lax.broadcasted_iota(jnp.int32, (16, WIDTH), 0) % 4
    hi = jnp.where(row < 2, len_ref[0] // 64, len_ref[1] // 64)
    lo = jnp.where(row < 2, len_ref[0] % 64, len_ref[1] % 64)
    qall[z, c, 0:8] = q_ref[...]
    qall[z, c, 8] = jnp.where(row % 2 == 0, hi, lo).astype(F32).astype(BF16)
    rowtab[g, y] = jnp.full((1, WIDTH), owner_ref[0] * 4 + block_ref[0], jnp.int32)
    pl.semaphore_wait(barrier, len(peers))

    sent = []
    spread, hand = {}, []

    def pass_on(o):
        came = qall.at[(z - o + NZ) % NZ, c]
        for k in BELOW[o]:
            i = PLACE[k]
            spread[k] = send(came, came, a_ss.at[i], a_rs.at[i], at(0, k - o, 0, 0))
            spread[k].start()
        i = PLACE.get(o, len(PLACE))
        hand.append(send(came, came, h_ss.at[i], h_rs.at[i], at(0, 0, 1, 0)))
        hand[-1].start()

    def arrive(*places):
        for o in places:
            spread[o].wait_recv()
            pass_on(o)

    pass_on(0)
    tables = []
    for i in range(NY - 1):
        tables.append(send(rowtab.at[g, y], rowtab.at[g, y], y_ss.at[i], y_rs.at[i], at(0, 0, 0, i + 1)))
        tables[-1].start()
    for t in tables:
        t.wait_recv()
    along_x, across = [], []
    for i, dx in enumerate(X_PEERS):
        along_x.append(send(rowtab.at[g], rowtab.at[g], t_ss.at[i], t_rs.at[i], at(dx, 0, 0, 0)))
        along_x[-1].start()

    def table_to_sibling(i, gg):
        across.append(send(rowtab.at[gg], rowtab.at[gg], w_ss.at[i], w_rs.at[i], at(0, 0, 1, 0)))
        across[-1].start()

    table_to_sibling(3, g)

    for r in range(2):
        qf = q_ref[4 * r : 4 * r + 4].reshape(ROWS, WIDTH).astype(F32)
        step = lax.broadcasted_iota(jnp.int32, (ROWS, 1), 0) // 16
        ss = []
        for b in range(4):
            k_b = fresh_ref[b].astype(F32)[r : r + 1, :WIDTH]
            s_b = jnp.sum(qf * k_b, axis=1, keepdims=True) * SCALE
            ss.append(jnp.where(step >= b, s_b, -jnp.inf))
        top = jnp.maximum(jnp.maximum(ss[0], ss[1]), jnp.maximum(ss[2], ss[3]))
        ws = [jnp.exp(s_b - top) for s_b in ss]
        total = ws[0] + ws[1] + ws[2] + ws[3]
        acc = jnp.zeros((ROWS, WIDTH), F32)
        for b in range(4):
            v_b = fresh_ref[b].astype(F32)[r : r + 1, WIDTH:]
            acc = acc + ws[b].astype(BF16).astype(F32) * v_b
        tail[r] = acc / total
        tail_lse[r] = jnp.broadcast_to(top + jnp.log(total), (ROWS, WIDTH))

    arrive(*ARRIVE[1])

    for s in range(SLOTS):
        kv_copies[s].wait()
        kt[s] = kv[s, :, :WIDTH].T

    arrive(*(o for o in ARRIVE[2] if BELOW[o]))
    for i, dx in enumerate(X_PEERS):
        along_x[i].wait_recv()
        table_to_sibling(i, ((x - dx + NX) % NX) * NC + c)
    arrive(*(o for o in ARRIVE[2] if not BELOW[o]))
    arrive(*(o for o in ARRIVE[3] if BELOW[o]))

    for t in across:
        t.wait_recv()
    lane = lax.broadcasted_iota(jnp.int32, (1, WIDTH), 1)
    want = (((x * NZ + (lane % 32) // 2) * NC + c) * 2 + lane % 2) * 4 + lane // 32
    index = jnp.zeros((1, WIDTH), jnp.int32)
    for gg in range(GROUPS):
        for s in range(SLOTS):
            index = jnp.where(rowtab[gg, s] == want, gg * SLOTS + s, index)
    ivec[...] = index
    to_smem = [
        pltpu.make_async_copy(rowtab, tab_s, sm_sem.at[0]),
        pltpu.make_async_copy(ivec, ivec_s, sm_sem.at[1]),
    ]
    for copy in to_smem:
        copy.start()
    for copy in to_smem:
        copy.wait()

    arrive(*(o for o in ARRIVE[3] if not BELOW[o]), *ARRIVE[4])
    for t in hand:
        t.wait_recv()

    group = lax.broadcasted_iota(jnp.int32, (16, WIDTH), 0) // 4
    got = (got0, got1)

    def choose(gg, half, ref):
        lens = jnp.zeros((16, WIDTH), F32)
        for i in range(2):
            owner = tab_s[gg, 2 * half + i, 0, 0] // 4
            zz, cc, r = (owner // 4) % NZ, (owner // 2) % NC, owner % 2
            ref[4 * i : 4 * i + 4] = qall[zz, cc, pl.ds(4 * r, 4)]
            lens = jnp.where(group == i, qall[zz, cc, 8].astype(F32), lens)
        ref[8] = lens.astype(BF16)

    queries = []
    for half in range(2):
        for i, dx in enumerate(X_PEERS):
            choose(((x + dx) % NX) * NC + c, half, sel.at[i, half])
            copy = send(
                sel.at[i, half], got[half].at[x], s_ss.at[i, half], s_rs.at[i, half], at(dx, 0, 0, 0)
            )
            copy.start()
            queries.append(copy)
        choose(g, half, got[half].at[x])

    lane_pos = lax.broadcasted_iota(jnp.int32, (1, BLOCK), 1).astype(F32)
    lane_id = lax.broadcasted_iota(jnp.int32, (ROWS, WIDTH), 1)
    lcols = jnp.zeros((ROWS, WIDTH), F32)
    back, lse_sent = [], []
    for half in range(2):
        for t in queries[half * len(X_PEERS) : (half + 1) * len(X_PEERS)]:
            t.wait_recv()
        rounded, totals = [], []
        for n in range(2):
            s = 2 * half + n
            code = tab_s[g, s, 0, 0]
            owner, blk = code // 4, code % 4
            src = owner // 64
            r = owner % 2
            q = got[half][src, 4 * n : 4 * n + 4].reshape(ROWS, WIDTH)
            lens = got[half][src, 8].astype(F32)
            hi = jnp.where(r == 0, lens[4 * n : 4 * n + 1], lens[4 * n + 2 : 4 * n + 3])
            lo = jnp.where(r == 0, lens[4 * n + 1 : 4 * n + 2], lens[4 * n + 3 : 4 * n + 4])
            left = (hi * 64.0 + lo)[:, :1] - (blk * BLOCK).astype(F32)
            scores = jnp.dot(q, kt[s], preferred_element_type=F32)
            scores = jnp.where(lane_pos < left, scores, -jnp.inf)
            top = jnp.max(scores, axis=1, keepdims=True)
            weights = jnp.exp2((scores - top) * (SCALE * LOG2E))
            total = jnp.sum(weights, axis=1, keepdims=True)
            lcols = jnp.where(lane_id == s, top * SCALE + jnp.log(total), lcols)
            rounded.append(weights.astype(BF16))
            totals.append(total)
        if half == 1:
            lt = jnp.concatenate([lcols, lcols], axis=0).T
            for s in range(SLOTS):
                lses[g, s] = lt[s : s + 1]
            for i in range(4):
                to = at(X_PEERS[i], 0, 0, 0) if i < 3 else at(0, 0, 1, 0)
                copy = send(lses.at[g], lses.at[g], l_ss.at[i], l_rs.at[i], to)
                copy.start()
                lse_sent.append(copy)
        for n in range(2):
            s = 2 * half + n
            part = jnp.dot(rounded[n], kv[s, :, WIDTH:], preferred_element_type=F32) / totals[n]
            parts[g, s] = part.astype(BF16).reshape(4, 16, WIDTH)
        mine = parts.at[g, 2 * half : 2 * half + 2]
        for i in range(4):
            to = at(X_PEERS[i], 0, 0, 0) if i < 3 else at(0, 0, 1, 0)
            copy = send(mine, mine, p_ss.at[i, half], p_rs.at[i, half], to)
            copy.start()
            back.append(copy)
    for copy in [*spread.values(), *hand, *tables, *along_x, *across, *queries]:
        copy.wait_send()

    handed = []

    def hand_parts(half):
        for i, dx in enumerate(X_PEERS):
            back[half * 4 + i].wait_recv()
            there = parts.at[((x - dx + NX) % NX) * NC + c, 2 * half : 2 * half + 2]
            copy = send(there, there, u_ss.at[i, half], u_rs.at[i, half], at(0, 0, 1, 0))
            copy.start()
            handed.append(copy)

    hand_parts(0)
    lse_handed = []
    for i, dx in enumerate(X_PEERS):
        lse_sent[i].wait_recv()
        there = lses.at[((x - dx + NX) % NX) * NC + c]
        copy = send(there, there, v_ss.at[i], v_rs.at[i], at(0, 0, 1, 0))
        copy.start()
        lse_handed.append(copy)
    hand_parts(1)
    lse_sent[3].wait_recv()
    for copy in lse_handed:
        copy.wait_recv()

    wmat[...] = jnp.zeros((WIDTH, WIDTH), F32)
    away = lax.broadcasted_iota(jnp.int32, (NZ, WIDTH), 0)
    half = lax.broadcasted_iota(jnp.int32, (NZ, WIDTH), 1) // ROWS
    target = (((x * NZ + (z + away) % NZ) * NC + c) * 2 + half) * 4
    ls = [jnp.full((NZ, WIDTH), NEG, F32) for _ in range(3)]
    for gg in range(GROUPS):
        for s in range(SLOTS):
            here = rowtab[gg, s] - target
            lse = lses[gg, s]
            ls = [jnp.where(here == k, lse, ls[k]) for k in range(3)]
    peak = jnp.maximum(jnp.maximum(ls[0], ls[1]), ls[2])
    ws = [jnp.exp(l - peak) for l in ls]
    total = ws[0] + ws[1] + ws[2]
    merged = peak + jnp.log(total)
    for k in range(3):
        wmat[16 * k : 16 * (k + 1)] = ws[k] / total
    for d in range(NZ):
        clse[d] = merged[d : d + 1]
    wcol[...] = wmat[...].T

    def build(d):
        d = d % NZ
        for r in range(2):
            acc = jnp.zeros((ROWS, WIDTH), F32)
            for k in range(3):
                i = ivec_s[0, k * 32 + ((z + d) % NZ) * 2 + r]
                p = parts[i // 4, i % 4].reshape(ROWS, WIDTH).astype(F32)
                acc = acc + wcol[r * ROWS : (r + 1) * ROWS, k * 16 + d : k * 16 + d + 1] * p
            cbuf[d, 4 * r : 4 * r + 4] = acc.astype(BF16).reshape(4, 16, WIDTH)

    for half in range(2):
        back[half * 4 + 3].wait_recv()
    for copy in handed:
        copy.wait_recv()

    up = {}

    def start_up(o, data, lse):
        i = PLACE[o]
        to = at(0, PARENT[o] - o, 0, 0)
        up[o] = (
            send(lse, rlse.at[i], d_ss.at[i], d_rs.at[i], to),
            send(data, rbuf.at[i], c_ss.at[i], c_rs.at[i], to),
        )

    for o in LEAVES:
        build(-o)
        start_up(o, cbuf.at[-o % NZ], clse.at[-o % NZ])
        for copy in up[o]:
            copy.start()
    for o in (*HUBS, 0):
        build(-o)
    for copy in [*back, *lse_sent, *handed, *lse_handed]:
        copy.wait_send()

    def merge(hubs):
        columns = {}
        for o in hubs:
            for k in CHILDREN[o]:
                up[k][0].wait_recv()
            ls = [clse[-o % NZ]] + [rlse[PLACE[k]] for k in CHILDREN[o]]
            peak = ls[0]
            for l in ls[1:]:
                peak = jnp.maximum(peak, l)
            ws = [jnp.exp(l - peak) for l in ls]
            total = ws[0]
            for w in ws[1:]:
                total = total + w
            n = HUBS.index(o)
            mlse[n] = peak + jnp.log(total)
            start_up(o, mbuf.at[n], mlse.at[n])
            up[o][0].start()
            for i, w in enumerate(ws):
                wmat[i : i + 1] = w / total
            columns[o] = wmat[0:8].T
        for o in hubs:
            for k in CHILDREN[o]:
                up[k][1].wait_recv()
            data = [cbuf[-o % NZ]] + [rbuf[PLACE[k]] for k in CHILDREN[o]]
            acc = jnp.zeros((WIDTH, WIDTH), F32)
            for i, p in enumerate(data):
                acc = acc + columns[o][:, i : i + 1] * p.reshape(WIDTH, WIDTH).astype(F32)
            mbuf[HUBS.index(o)] = acc.astype(BF16).reshape(8, 16, WIDTH)
            up[o][1].start()

    for n in sorted({height(PARENT, o) for o in HUBS}):
        merge([o for o in HUBS if height(PARENT, o) == n])
    for o in up:
        if PARENT[o] != 0:
            for copy in up[o]:
                copy.wait_send()

    for k in CHILDREN[0]:
        up[k][0].wait_recv()
    for i, k in enumerate(CHILDREN[0]):
        wmat[i : i + 1] = rlse[PLACE[k]]
    wmat[len(CHILDREN[0]) : len(CHILDREN[0]) + 1] = clse[0]
    wt = wmat[0:8].T
    ends = []
    for r in range(2):
        rs = slice(r * ROWS, (r + 1) * ROWS)
        tl = tail_lse[r][:, :1]
        ls = [wt[rs, n : n + 1] for n in range(len(CHILDREN[0]) + 1)]
        peak = tl
        for l in ls:
            peak = jnp.maximum(peak, l)
        w = jnp.exp(tl - peak)
        ws = [jnp.exp(l - peak) for l in ls]
        denom = w
        for v in ws:
            denom = denom + v
        p = cbuf[0, 4 * r : 4 * r + 4].reshape(ROWS, WIDTH).astype(F32)
        ends.append((ws, denom, w * tail[r] + ws[-1] * p))
    for k in CHILDREN[0]:
        up[k][1].wait_recv()
    done = []
    for r in range(2):
        ws, denom, acc = ends[r]
        for n, k in enumerate(CHILDREN[0]):
            acc = acc + ws[n] * rbuf[PLACE[k], 4 * r : 4 * r + 4].reshape(ROWS, WIDTH).astype(F32)
        done.append(acc / denom)
    for a in range(4):
        heads = [
            jnp.concatenate([done[0][i : i + 1], done[1][i : i + 1]], axis=0)
            for i in range(16 * a, 16 * a + 16)
        ]
        out_ref[a] = jnp.concatenate(heads, axis=1).astype(BF16)

    for o in CHILDREN[0]:
        for copy in up[o]:
            copy.wait_send()


def shards(query, fresh_key_value, kv_pool, lengths, slot_owner, slot_block):
    dma = pltpu.SemaphoreType.DMA
    hbm = pl.BlockSpec(memory_space=pl.ANY)
    m = len(PARENT)
    return pl.pallas_call(
        kernel,
        out_shape=jax.ShapeDtypeStruct(query.shape, BF16),
        in_specs=[hbm] * 6,
        out_specs=pl.BlockSpec(memory_space=pltpu.VMEM),
        scratch_shapes=[
            pltpu.VMEM(query.shape, BF16),
            pltpu.VMEM((8, 16, WIDTH), BF16),
            pltpu.VMEM(fresh_key_value.shape, BF16),
            pltpu.SMEM(lengths.shape, jnp.int32),
            pltpu.SMEM(slot_owner.shape, jnp.int32),
            pltpu.SMEM(slot_block.shape, jnp.int32),
            pltpu.VMEM((SLOTS, BLOCK, 2 * WIDTH), BF16),
            pltpu.VMEM((SLOTS, WIDTH, BLOCK), BF16),
            pltpu.VMEM((NZ, NC, 9, 16, WIDTH), BF16),
            pltpu.VMEM((GROUPS, SLOTS, 1, WIDTH), jnp.int32),
            pltpu.VMEM((1, WIDTH), jnp.int32),
            pltpu.SMEM((GROUPS, SLOTS, 1, WIDTH), jnp.int32),
            pltpu.SMEM((1, WIDTH), jnp.int32),
            pltpu.VMEM((3, 2, 9, 16, WIDTH), BF16),
            pltpu.VMEM((NX, 9, 16, WIDTH), BF16),
            pltpu.VMEM((NX, 9, 16, WIDTH), BF16),
            pltpu.VMEM((GROUPS, SLOTS, 4, 16, WIDTH), BF16),
            pltpu.VMEM((GROUPS, SLOTS, 1, WIDTH), F32),
            pltpu.VMEM((WIDTH, WIDTH), F32),
            pltpu.VMEM((WIDTH, WIDTH), F32),
            pltpu.VMEM((NZ, 8, 16, WIDTH), BF16),
            pltpu.VMEM((NZ, 1, WIDTH), F32),
            pltpu.VMEM((m, 8, 16, WIDTH), BF16),
            pltpu.VMEM((m, 1, WIDTH), F32),
            pltpu.VMEM((len(HUBS), 8, 16, WIDTH), BF16),
            pltpu.VMEM((len(HUBS), 1, WIDTH), F32),
            pltpu.VMEM((2, ROWS, WIDTH), F32),
            pltpu.VMEM((2, ROWS, WIDTH), F32),
            dma((5,)),
            dma((SLOTS,)),
            dma((2,)),
            dma((3,)), dma((3,)),
            dma((3,)), dma((3,)),
            dma((4,)), dma((4,)),
            dma((m,)), dma((m,)),
            dma((m + 1,)), dma((m + 1,)),
            dma((3, 2)), dma((3, 2)),
            dma((4, 2)), dma((4, 2)),
            dma((4,)), dma((4,)),
            dma((3, 2)), dma((3, 2)),
            dma((3,)), dma((3,)),
            dma((m,)), dma((m,)),
            dma((m,)), dma((m,)),
        ],
        compiler_params=pltpu.CompilerParams(
            collective_id=0, has_side_effects=True, vmem_limit_bytes=60 << 20
        ),
        name="lent_attention",
    )(query, fresh_key_value, kv_pool, lengths, slot_owner, slot_block)


def solution(mesh):
    placed = (
        P(None, "inst", "tp"),
        P(None, "inst", "tp"),
        P("inst", None, "tp"),
        P("inst"),
        P(("inst", "tp")),
        P(("inst", "tp")),
    )
    return jax.shard_map(
        shards, mesh=mesh, in_specs=placed, out_specs=P(None, "inst", "tp"), check_vma=False
    )
```

```python
import math

import jax
import jax.numpy as jnp
from jax import lax
from jax.experimental import pallas as pl
from jax.experimental.pallas import tpu as pltpu
from jax.sharding import PartitionSpec as P

BLOCK = 2048
WIDTH = 128
ROWS = 64
NX, NZ, NC, NY = 4, 16, 2, 4
GROUPS = NX * NC
SLOTS = 4
SCALE = 1.0 / math.sqrt(WIDTH)
LOG2E = math.log2(math.e)
NEG = -1e30
F32 = jnp.float32
BF16 = jnp.bfloat16

DOWN = {3: 0, -3: 0, 1: 0, -1: 0, 6: 3, 2: 3, 4: 3, -6: -3, -2: -3, -4: -3, 8: 6, 7: 6, 5: 6, -7: -6, -5: -6}
PARENT = {3: 0, -3: 0, 1: 0, -1: 0, 6: 3, 2: 3, 4: 3, -6: -3, -2: -3, -4: -3, 8: 6, 7: 6, 5: 6, -7: -6, -5: -6}


def level(tree, o):
    return 0 if o == 0 else 1 + level(tree, tree[o])


def height(tree, o):
    return max([0] + [1 + height(tree, k) for k in tree if tree[k] == o])


BELOW = {p: [o for o in DOWN if DOWN[o] == p] for p in (0, *DOWN)}
CHILDREN = {p: [o for o in PARENT if PARENT[o] == p] for p in (0, *PARENT)}
PLACE = {o: i for i, o in enumerate(PARENT)}
ARRIVE = {n: sorted((o for o in DOWN if level(DOWN, o) == n), key=lambda o: (-height(DOWN, o), abs(o))) for n in range(1, 5)}
LEAVES = sorted((o for o in PARENT if not CHILDREN[o]), key=lambda o: -level(PARENT, o))
HUBS = sorted((o for o in PARENT if CHILDREN[o]), key=lambda o: height(PARENT, o))
NEAR = sorted({t * (o - tree[o]) for tree in (DOWN, PARENT) for o in tree for t in (1, -1)}, key=lambda d: -abs(d))
X_PEERS = (2, 1, 3)


def kernel(
    q_in, fresh_in, kv_ref, len_in, owner_in, block_in, out_ref,
    q_raw, q_ref, fresh_ref, len_ref, owner_ref, block_ref,
    kv, kt, qall, rowtab, ivec, tab_s, ivec_s, sel, got0, got1, parts, lses, wmat, wcol,
    cbuf, clse, rbuf, rlse, mbuf, mlse, tail, tail_lse,
    in_sem, kv_sem, sm_sem, y_ss, y_rs, t_ss, t_rs, w_ss, w_rs, a_ss, a_rs, h_ss, h_rs, s_ss, s_rs,
    p_ss, p_rs, l_ss, l_rs, u_ss, u_rs, c_ss, c_rs, d_ss, d_rs,
):
    me = lax.axis_index("inst")
    y = lax.axis_index("tp")
    x, z, c = me // (NZ * NC), (me // NC) % NZ, me % NC
    g = x * NC + c

    def at(dx, dz, dc, dy):
        xx, zz = (x + dx + NX) % NX, (z + dz + NZ) % NZ
        cc, yy = (c + dc) % NC, (y + dy) % NY
        return ((xx * NZ + zz) * NC + cc, yy)

    def send(src, dst, ss, rs, to):
        return pltpu.make_async_remote_copy(
            src_ref=src, dst_ref=dst, send_sem=ss, recv_sem=rs,
            device_id=to, device_id_type=pl.DeviceIdType.MESH,
        )

    peers = [at(0, d, 0, 0) for d in NEAR]
    row = [at(dx, 0, 0, 0) for dx in X_PEERS] + [at(0, 0, 1, 0)] + [at(dx, 0, 1, 0) for dx in X_PEERS]
    peers += row
    peers += [at(0, 0, 0, d) for d in range(1, NY)]
    barrier = pltpu.get_barrier_semaphore()
    for p in peers:
        pl.semaphore_signal(barrier, inc=1, device_id=p, device_id_type=pl.DeviceIdType.MESH)
    inputs = [
        pltpu.make_async_copy(a, b, in_sem.at[i])
        for i, (a, b) in enumerate(
            ((q_in, q_raw), (len_in, len_ref), (owner_in, owner_ref), (block_in, block_ref), (fresh_in, fresh_ref))
        )
    ]
    for copy in inputs:
        copy.start()
    kv_copies = [pltpu.make_async_copy(kv_ref.at[s], kv.at[s], kv_sem.at[s]) for s in range(SLOTS)]
    for copy in kv_copies:
        copy.start()
    for copy in inputs:
        copy.wait()
    for a in range(4):
        qa = q_raw[a].astype(F32)
        for r in range(2):
            tile = jnp.concatenate([qa[r : r + 1, WIDTH * h : WIDTH * (h + 1)] for h in range(16)], axis=0)
            q_ref[4 * r + a] = tile.astype(BF16)
    line = lax.broadcasted_iota(jnp.int32, (16, WIDTH), 0) % 4
    hi = jnp.where(line < 2, len_ref[0] // 64, len_ref[1] // 64)
    lo = jnp.where(line < 2, len_ref[0] % 64, len_ref[1] % 64)
    qall[z, c, 0:8] = q_ref[...]
    qall[z, c, 8] = jnp.where(line % 2 == 0, hi, lo).astype(F32).astype(BF16)
    rowtab[g, y] = jnp.full((1, WIDTH), owner_ref[0] * 4 + block_ref[0], jnp.int32)
    pl.semaphore_wait(barrier, len(peers))

    sent = []
    spread, hand = {}, []

    def pass_on(o):
        came = qall.at[(z - o + NZ) % NZ, c]
        for k in BELOW[o]:
            i = PLACE[k]
            spread[k] = send(came, came, a_ss.at[i], a_rs.at[i], at(0, k - o, 0, 0))
            spread[k].start()
        i = PLACE.get(o, len(PLACE))
        hand.append(send(came, came, h_ss.at[i], h_rs.at[i], at(0, 0, 1, 0)))
        hand[-1].start()

    def arrive(*places):
        for o in places:
            spread[o].wait_recv()
            pass_on(o)

    pass_on(0)
    tables = []
    for i in range(NY - 1):
        tables.append(send(rowtab.at[g, y], rowtab.at[g, y], y_ss.at[i], y_rs.at[i], at(0, 0, 0, i + 1)))
        tables[-1].start()
    for t in tables:
        t.wait_recv()
    along_x, across = [], []
    for i, dx in enumerate(X_PEERS):
        along_x.append(send(rowtab.at[g], rowtab.at[g], t_ss.at[i], t_rs.at[i], at(dx, 0, 0, 0)))
        along_x[-1].start()

    def table_to_sibling(i, gg):
        across.append(send(rowtab.at[gg], rowtab.at[gg], w_ss.at[i], w_rs.at[i], at(0, 0, 1, 0)))
        across[-1].start()

    table_to_sibling(3, g)

    for r in range(2):
        qf = q_ref[4 * r : 4 * r + 4].reshape(ROWS, WIDTH).astype(F32)
        step = lax.broadcasted_iota(jnp.int32, (ROWS, 1), 0) // 16
        ss = []
        for b in range(4):
            k_b = fresh_ref[b].astype(F32)[r : r + 1, :WIDTH]
            s_b = jnp.sum(qf * k_b, axis=1, keepdims=True) * SCALE
            ss.append(jnp.where(step >= b, s_b, -jnp.inf))
        top = jnp.maximum(jnp.maximum(ss[0], ss[1]), jnp.maximum(ss[2], ss[3]))
        ws = [jnp.exp(s_b - top) for s_b in ss]
        total = ws[0] + ws[1] + ws[2] + ws[3]
        acc = jnp.zeros((ROWS, WIDTH), F32)
        for b in range(4):
            v_b = fresh_ref[b].astype(F32)[r : r + 1, WIDTH:]
            acc = acc + ws[b].astype(BF16).astype(F32) * v_b
        tail[r] = acc / total
        tail_lse[r] = jnp.broadcast_to(top + jnp.log(total), (ROWS, WIDTH))

    arrive(*ARRIVE[1])

    for s in range(SLOTS):
        kv_copies[s].wait()
        kt[s] = kv[s, :, :WIDTH].T

    arrive(*(o for o in ARRIVE[2] if BELOW[o]))
    for i, dx in enumerate(X_PEERS):
        along_x[i].wait_recv()
        table_to_sibling(i, ((x - dx + NX) % NX) * NC + c)
    arrive(*(o for o in ARRIVE[2] if not BELOW[o]))
    arrive(*(o for o in ARRIVE[3] if BELOW[o]))

    for t in across:
        t.wait_recv()
    lane = lax.broadcasted_iota(jnp.int32, (1, WIDTH), 1)
    want = (((x * NZ + (lane % 32) // 2) * NC + c) * 2 + lane % 2) * 4 + lane // 32
    index = jnp.zeros((1, WIDTH), jnp.int32)
    for gg in range(GROUPS):
        for s in range(SLOTS):
            index = jnp.where(rowtab[gg, s] == want, gg * SLOTS + s, index)
    ivec[...] = index
    to_smem = [
        pltpu.make_async_copy(rowtab, tab_s, sm_sem.at[0]),
        pltpu.make_async_copy(ivec, ivec_s, sm_sem.at[1]),
    ]
    for copy in to_smem:
        copy.start()
    for copy in to_smem:
        copy.wait()

    arrive(*(o for o in ARRIVE[3] if not BELOW[o]), *ARRIVE[4])
    for t in hand:
        t.wait_recv()

    group = lax.broadcasted_iota(jnp.int32, (16, WIDTH), 0) // 4
    got = (got0, got1)

    def choose(gg, half, ref):
        lens = jnp.zeros((16, WIDTH), F32)
        for i in range(2):
            owner = tab_s[gg, 2 * half + i, 0, 0] // 4
            zz, cc, r = (owner // 4) % NZ, (owner // 2) % NC, owner % 2
            ref[4 * i : 4 * i + 4] = qall[zz, cc, pl.ds(4 * r, 4)]
            lens = jnp.where(group == i, qall[zz, cc, 8].astype(F32), lens)
        ref[8] = lens.astype(BF16)

    queries = []
    for half in range(2):
        for i, dx in enumerate(X_PEERS):
            choose(((x + dx) % NX) * NC + c, half, sel.at[i, half])
            copy = send(
                sel.at[i, half], got[half].at[x], s_ss.at[i, half], s_rs.at[i, half], at(dx, 0, 0, 0)
            )
            copy.start()
            queries.append(copy)
        choose(g, half, got[half].at[x])

    lane_pos = lax.broadcasted_iota(jnp.int32, (1, BLOCK), 1).astype(F32)
    lane_id = lax.broadcasted_iota(jnp.int32, (ROWS, WIDTH), 1)
    lcols = jnp.zeros((ROWS, WIDTH), F32)
    back, lse_sent = [], []
    for half in range(2):
        for t in queries[half * len(X_PEERS) : (half + 1) * len(X_PEERS)]:
            t.wait_recv()
        rounded, totals = [], []
        for n in range(2):
            s = 2 * half + n
            code = tab_s[g, s, 0, 0]
            owner, blk = code // 4, code % 4
            src = owner // 64
            r = owner % 2
            q = got[half][src, 4 * n : 4 * n + 4].reshape(ROWS, WIDTH)
            lens = got[half][src, 8].astype(F32)
            hi = jnp.where(r == 0, lens[4 * n : 4 * n + 1], lens[4 * n + 2 : 4 * n + 3])
            lo = jnp.where(r == 0, lens[4 * n + 1 : 4 * n + 2], lens[4 * n + 3 : 4 * n + 4])
            left = (hi * 64.0 + lo)[:, :1] - (blk * BLOCK).astype(F32)
            scores = jnp.dot(q, kt[s], preferred_element_type=F32)
            scores = jnp.where(lane_pos < left, scores, -jnp.inf)
            top = jnp.max(scores, axis=1, keepdims=True)
            weights = jnp.exp2((scores - top) * (SCALE * LOG2E))
            total = jnp.sum(weights, axis=1, keepdims=True)
            lcols = jnp.where(lane_id == s, top * SCALE + jnp.log(total), lcols)
            rounded.append(weights.astype(BF16))
            totals.append(total)
        if half == 1:
            lt = jnp.concatenate([lcols, lcols], axis=0).T
            for s in range(SLOTS):
                lses[g, s] = lt[s : s + 1]
            for i, to in enumerate(row):
                copy = send(lses.at[g], lses.at[g], l_ss.at[i], l_rs.at[i], to)
                copy.start()
                lse_sent.append(copy)
        for n in range(2):
            s = 2 * half + n
            part = jnp.dot(rounded[n], kv[s, :, WIDTH:], preferred_element_type=F32) / totals[n]
            parts[g, s] = part.astype(BF16).reshape(4, 16, WIDTH)
        mine = parts.at[g, 2 * half : 2 * half + 2]
        for i, to in enumerate(row if half else row[:4]):
            copy = send(mine, mine, p_ss.at[i, half], p_rs.at[i, half], to)
            copy.start()
            back.append(copy)
    for copy in [*spread.values(), *hand, *tables, *along_x, *across, *queries]:
        copy.wait_send()

    handed = []
    for i, dx in enumerate(X_PEERS):
        back[i].wait_recv()
        there = parts.at[((x - dx + NX) % NX) * NC + c, 0:2]
        copy = send(there, there, u_ss.at[i], u_rs.at[i], at(0, 0, 1, 0))
        copy.start()
        handed.append(copy)
    for copy in lse_sent:
        copy.wait_recv()

    wmat[...] = jnp.zeros((WIDTH, WIDTH), F32)
    away = lax.broadcasted_iota(jnp.int32, (NZ, WIDTH), 0)
    half = lax.broadcasted_iota(jnp.int32, (NZ, WIDTH), 1) // ROWS
    target = (((x * NZ + (z + away) % NZ) * NC + c) * 2 + half) * 4
    ls = [jnp.full((NZ, WIDTH), NEG, F32) for _ in range(3)]
    for gg in range(GROUPS):
        for s in range(SLOTS):
            here = rowtab[gg, s] - target
            lse = lses[gg, s]
            ls = [jnp.where(here == k, lse, ls[k]) for k in range(3)]
    peak = jnp.maximum(jnp.maximum(ls[0], ls[1]), ls[2])
    ws = [jnp.exp(l - peak) for l in ls]
    total = ws[0] + ws[1] + ws[2]
    merged = peak + jnp.log(total)
    for k in range(3):
        wmat[16 * k : 16 * (k + 1)] = ws[k] / total
    for d in range(NZ):
        clse[d] = merged[d : d + 1]
    wcol[...] = wmat[...].T

    def build(d):
        d = d % NZ
        for r in range(2):
            acc = jnp.zeros((ROWS, WIDTH), F32)
            for k in range(3):
                i = ivec_s[0, k * 32 + ((z + d) % NZ) * 2 + r]
                p = parts[i // 4, i % 4].reshape(ROWS, WIDTH).astype(F32)
                acc = acc + wcol[r * ROWS : (r + 1) * ROWS, k * 16 + d : k * 16 + d + 1] * p
            cbuf[d, 4 * r : 4 * r + 4] = acc.astype(BF16).reshape(4, 16, WIDTH)

    for copy in back[3:] + handed:
        copy.wait_recv()

    up = {}

    def start_up(o, data, lse):
        i = PLACE[o]
        to = at(0, PARENT[o] - o, 0, 0)
        up[o] = (
            send(lse, rlse.at[i], d_ss.at[i], d_rs.at[i], to),
            send(data, rbuf.at[i], c_ss.at[i], c_rs.at[i], to),
        )

    now = [o for o in LEAVES if PARENT[o] != 0]
    later = [o for o in LEAVES if o not in now]
    for o in now:
        build(-o)
        start_up(o, cbuf.at[-o % NZ], clse.at[-o % NZ])
        for copy in up[o]:
            copy.start()
    for o in (*HUBS, 0, *later):
        build(-o)
    for copy in [*back, *lse_sent, *handed]:
        copy.wait_send()

    def merge(hubs):
        columns = {}
        for o in hubs:
            for k in CHILDREN[o]:
                up[k][0].wait_recv()
            ls = [clse[-o % NZ]] + [rlse[PLACE[k]] for k in CHILDREN[o]]
            peak = ls[0]
            for l in ls[1:]:
                peak = jnp.maximum(peak, l)
            ws = [jnp.exp(l - peak) for l in ls]
            total = ws[0]
            for w in ws[1:]:
                total = total + w
            n = HUBS.index(o)
            mlse[n] = peak + jnp.log(total)
            start_up(o, mbuf.at[n], mlse.at[n])
            up[o][0].start()
            for i, w in enumerate(ws):
                wmat[i : i + 1] = w / total
            columns[o] = wmat[0:8].T
        for o in hubs:
            for k in CHILDREN[o]:
                up[k][1].wait_recv()
            data = [cbuf[-o % NZ]] + [rbuf[PLACE[k]] for k in CHILDREN[o]]
            acc = jnp.zeros((WIDTH, WIDTH), F32)
            for i, p in enumerate(data):
                acc = acc + columns[o][:, i : i + 1] * p.reshape(WIDTH, WIDTH).astype(F32)
            mbuf[HUBS.index(o)] = acc.astype(BF16).reshape(8, 16, WIDTH)
            up[o][1].start()

    for n in sorted({height(PARENT, o) for o in HUBS}):
        merge([o for o in HUBS if height(PARENT, o) == n])
        if n == 1:
            for o in later:
                start_up(o, cbuf.at[-o % NZ], clse.at[-o % NZ])
                for copy in up[o]:
                    copy.start()
    for o in up:
        if PARENT[o] != 0:
            for copy in up[o]:
                copy.wait_send()

    for k in CHILDREN[0]:
        up[k][0].wait_recv()
    for i, k in enumerate(CHILDREN[0]):
        wmat[i : i + 1] = rlse[PLACE[k]]
    wmat[len(CHILDREN[0]) : len(CHILDREN[0]) + 1] = clse[0]
    wt = wmat[0:8].T
    ends = []
    for r in range(2):
        rs = slice(r * ROWS, (r + 1) * ROWS)
        tl = tail_lse[r][:, :1]
        ls = [wt[rs, n : n + 1] for n in range(len(CHILDREN[0]) + 1)]
        peak = tl
        for l in ls:
            peak = jnp.maximum(peak, l)
        w = jnp.exp(tl - peak)
        ws = [jnp.exp(l - peak) for l in ls]
        denom = w
        for v in ws:
            denom = denom + v
        p = cbuf[0, 4 * r : 4 * r + 4].reshape(ROWS, WIDTH).astype(F32)
        ends.append((ws, denom, w * tail[r] + ws[-1] * p))
    for k in CHILDREN[0]:
        up[k][1].wait_recv()
    done = []
    for r in range(2):
        ws, denom, acc = ends[r]
        for n, k in enumerate(CHILDREN[0]):
            acc = acc + ws[n] * rbuf[PLACE[k], 4 * r : 4 * r + 4].reshape(ROWS, WIDTH).astype(F32)
        done.append(acc / denom)
    for a in range(4):
        heads = [
            jnp.concatenate([done[0][i : i + 1], done[1][i : i + 1]], axis=0)
            for i in range(16 * a, 16 * a + 16)
        ]
        out_ref[a] = jnp.concatenate(heads, axis=1).astype(BF16)

    for o in CHILDREN[0]:
        for copy in up[o]:
            copy.wait_send()


def shards(query, fresh_key_value, kv_pool, lengths, slot_owner, slot_block):
    dma = pltpu.SemaphoreType.DMA
    hbm = pl.BlockSpec(memory_space=pl.ANY)
    m = len(PARENT)
    return pl.pallas_call(
        kernel,
        out_shape=jax.ShapeDtypeStruct(query.shape, BF16),
        in_specs=[hbm] * 6,
        out_specs=pl.BlockSpec(memory_space=pltpu.VMEM),
        scratch_shapes=[
            pltpu.VMEM(query.shape, BF16),
            pltpu.VMEM((8, 16, WIDTH), BF16),
            pltpu.VMEM(fresh_key_value.shape, BF16),
            pltpu.SMEM(lengths.shape, jnp.int32),
            pltpu.SMEM(slot_owner.shape, jnp.int32),
            pltpu.SMEM(slot_block.shape, jnp.int32),
            pltpu.VMEM((SLOTS, BLOCK, 2 * WIDTH), BF16),
            pltpu.VMEM((SLOTS, WIDTH, BLOCK), BF16),
            pltpu.VMEM((NZ, NC, 9, 16, WIDTH), BF16),
            pltpu.VMEM((GROUPS, SLOTS, 1, WIDTH), jnp.int32),
            pltpu.VMEM((1, WIDTH), jnp.int32),
            pltpu.SMEM((GROUPS, SLOTS, 1, WIDTH), jnp.int32),
            pltpu.SMEM((1, WIDTH), jnp.int32),
            pltpu.VMEM((3, 2, 9, 16, WIDTH), BF16),
            pltpu.VMEM((NX, 9, 16, WIDTH), BF16),
            pltpu.VMEM((NX, 9, 16, WIDTH), BF16),
            pltpu.VMEM((GROUPS, SLOTS, 4, 16, WIDTH), BF16),
            pltpu.VMEM((GROUPS, SLOTS, 1, WIDTH), F32),
            pltpu.VMEM((WIDTH, WIDTH), F32),
            pltpu.VMEM((WIDTH, WIDTH), F32),
            pltpu.VMEM((NZ, 8, 16, WIDTH), BF16),
            pltpu.VMEM((NZ, 1, WIDTH), F32),
            pltpu.VMEM((m, 8, 16, WIDTH), BF16),
            pltpu.VMEM((m, 1, WIDTH), F32),
            pltpu.VMEM((len(HUBS), 8, 16, WIDTH), BF16),
            pltpu.VMEM((len(HUBS), 1, WIDTH), F32),
            pltpu.VMEM((2, ROWS, WIDTH), F32),
            pltpu.VMEM((2, ROWS, WIDTH), F32),
            dma((5,)),
            dma((SLOTS,)),
            dma((2,)),
            dma((3,)), dma((3,)),
            dma((3,)), dma((3,)),
            dma((4,)), dma((4,)),
            dma((m,)), dma((m,)),
            dma((m + 1,)), dma((m + 1,)),
            dma((3, 2)), dma((3, 2)),
            dma((7, 2)), dma((7, 2)),
            dma((7,)), dma((7,)),
            dma((3,)), dma((3,)),
            dma((m,)), dma((m,)),
            dma((m,)), dma((m,)),
        ],
        compiler_params=pltpu.CompilerParams(
            collective_id=0, has_side_effects=True, vmem_limit_bytes=60 << 20
        ),
        name="lent_attention",
    )(query, fresh_key_value, kv_pool, lengths, slot_owner, slot_block)


def solution(mesh):
    placed = (
        P(None, "inst", "tp"),
        P(None, "inst", "tp"),
        P("inst", None, "tp"),
        P("inst"),
        P(("inst", "tp")),
        P(("inst", "tp")),
    )
    return jax.shard_map(
        shards, mesh=mesh, in_specs=placed, out_specs=P(None, "inst", "tp"), check_vma=False
    )
```

```python
import math

import jax
import jax.numpy as jnp
from jax import lax
from jax.experimental import pallas as pl
from jax.experimental.pallas import tpu as pltpu
from jax.sharding import PartitionSpec as P

BLOCK = 2048
WIDTH = 128
ROWS = 64
NX, NZ, NC, NY = 4, 16, 2, 4
GROUPS = NX * NC
SLOTS = 4
SCALE = 1.0 / math.sqrt(WIDTH)
LOG2E = math.log2(math.e)
NEG = -1e30
F32 = jnp.float32
BF16 = jnp.bfloat16

DOWN = {3: 0, -3: 0, 1: 0, -1: 0, 6: 3, 2: 3, 4: 3, -6: -3, -2: -3, -4: -3, 8: 6, 7: 6, 5: 6, -7: -6, -5: -6}
PARENT = {3: 0, -3: 0, 1: 0, -1: 0, 6: 3, 2: 3, 4: 3, -6: -3, -2: -3, -4: -3, 8: 6, 7: 6, 5: 6, -7: -6, -5: -6}


def level(tree, o):
    return 0 if o == 0 else 1 + level(tree, tree[o])


def height(tree, o):
    return max([0] + [1 + height(tree, k) for k in tree if tree[k] == o])


BELOW = {p: [o for o in DOWN if DOWN[o] == p] for p in (0, *DOWN)}
CHILDREN = {p: [o for o in PARENT if PARENT[o] == p] for p in (0, *PARENT)}
PLACE = {o: i for i, o in enumerate(PARENT)}
ARRIVE = {n: sorted((o for o in DOWN if level(DOWN, o) == n), key=lambda o: (-height(DOWN, o), abs(o))) for n in range(1, 5)}
LEAVES = sorted((o for o in PARENT if not CHILDREN[o]), key=lambda o: -level(PARENT, o))
HUBS = sorted((o for o in PARENT if CHILDREN[o]), key=lambda o: height(PARENT, o))
NEAR = sorted({t * (o - tree[o]) for tree in (DOWN, PARENT) for o in tree for t in (1, -1)}, key=lambda d: -abs(d))
X_PEERS = (2, 1, 3)


def kernel(
    q_in, fresh_in, kv_ref, len_in, owner_in, block_in, out_ref,
    q_raw, q_ref, fresh_ref, len_ref, owner_ref, block_ref,
    kv, kt, qall, rowtab, ivec, tab_s, ivec_s, sel, got0, got1, parts, lses, wmat, wcol,
    cbuf, clse, rbuf, rlse, mbuf, mlse, tail, tail_lse,
    in_sem, kv_sem, sm_sem, y_ss, y_rs, t_ss, t_rs, w_ss, w_rs, a_ss, a_rs, h_ss, h_rs, s_ss, s_rs,
    p_ss, p_rs, l_ss, l_rs, u_ss, u_rs, c_ss, c_rs, d_ss, d_rs,
):
    me = lax.axis_index("inst")
    y = lax.axis_index("tp")
    x, z, c = me // (NZ * NC), (me // NC) % NZ, me % NC
    g = x * NC + c

    def at(dx, dz, dc, dy):
        xx, zz = (x + dx + NX) % NX, (z + dz + NZ) % NZ
        cc, yy = (c + dc) % NC, (y + dy) % NY
        return ((xx * NZ + zz) * NC + cc, yy)

    def send(src, dst, ss, rs, to):
        return pltpu.make_async_remote_copy(
            src_ref=src, dst_ref=dst, send_sem=ss, recv_sem=rs,
            device_id=to, device_id_type=pl.DeviceIdType.MESH,
        )

    peers = [at(0, d, 0, 0) for d in NEAR]
    row = [at(dx, 0, 0, 0) for dx in X_PEERS] + [at(0, 0, 1, 0)] + [at(dx, 0, 1, 0) for dx in X_PEERS]
    peers += row
    peers += [at(0, 0, 0, d) for d in range(1, NY)]
    barrier = pltpu.get_barrier_semaphore()
    for p in peers:
        pl.semaphore_signal(barrier, inc=1, device_id=p, device_id_type=pl.DeviceIdType.MESH)
    inputs = [
        pltpu.make_async_copy(a, b, in_sem.at[i])
        for i, (a, b) in enumerate(
            ((q_in, q_raw), (len_in, len_ref), (owner_in, owner_ref), (block_in, block_ref), (fresh_in, fresh_ref))
        )
    ]
    for copy in inputs:
        copy.start()
    kv_copies = [pltpu.make_async_copy(kv_ref.at[s], kv.at[s], kv_sem.at[s]) for s in range(SLOTS)]
    for copy in kv_copies:
        copy.start()
    for copy in inputs:
        copy.wait()
    for a in range(4):
        qa = q_raw[a].astype(F32)
        for r in range(2):
            tile = jnp.concatenate([qa[r : r + 1, WIDTH * h : WIDTH * (h + 1)] for h in range(16)], axis=0)
            q_ref[4 * r + a] = tile.astype(BF16)
    line = lax.broadcasted_iota(jnp.int32, (16, WIDTH), 0) % 4
    hi = jnp.where(line < 2, len_ref[0] // 64, len_ref[1] // 64)
    lo = jnp.where(line < 2, len_ref[0] % 64, len_ref[1] % 64)
    qall[z, c, 0:8] = q_ref[...]
    qall[z, c, 8] = jnp.where(line % 2 == 0, hi, lo).astype(F32).astype(BF16)
    rowtab[g, y] = jnp.full((1, WIDTH), owner_ref[0] * 4 + block_ref[0], jnp.int32)
    pl.semaphore_wait(barrier, len(peers))

    sent = []
    spread, hand = {}, []

    def pass_on(o):
        came = qall.at[(z - o + NZ) % NZ, c]
        for k in BELOW[o]:
            i = PLACE[k]
            spread[k] = send(came, came, a_ss.at[i], a_rs.at[i], at(0, k - o, 0, 0))
            spread[k].start()
        i = PLACE.get(o, len(PLACE))
        hand.append(send(came, came, h_ss.at[i], h_rs.at[i], at(0, 0, 1, 0)))
        hand[-1].start()

    def arrive(*places):
        for o in places:
            spread[o].wait_recv()
            pass_on(o)

    pass_on(0)
    tables = []
    for i in range(NY - 1):
        tables.append(send(rowtab.at[g, y], rowtab.at[g, y], y_ss.at[i], y_rs.at[i], at(0, 0, 0, i + 1)))
        tables[-1].start()
    for t in tables:
        t.wait_recv()
    along_x, across = [], []
    for i, dx in enumerate(X_PEERS):
        along_x.append(send(rowtab.at[g], rowtab.at[g], t_ss.at[i], t_rs.at[i], at(dx, 0, 0, 0)))
        along_x[-1].start()

    def table_to_sibling(i, gg):
        across.append(send(rowtab.at[gg], rowtab.at[gg], w_ss.at[i], w_rs.at[i], at(0, 0, 1, 0)))
        across[-1].start()

    table_to_sibling(3, g)

    for r in range(2):
        qf = q_ref[4 * r : 4 * r + 4].reshape(ROWS, WIDTH).astype(F32)
        step = lax.broadcasted_iota(jnp.int32, (ROWS, 1), 0) // 16
        ss = []
        for b in range(4):
            k_b = fresh_ref[b].astype(F32)[r : r + 1, :WIDTH]
            s_b = jnp.sum(qf * k_b, axis=1, keepdims=True) * SCALE
            ss.append(jnp.where(step >= b, s_b, -jnp.inf))
        top = jnp.maximum(jnp.maximum(ss[0], ss[1]), jnp.maximum(ss[2], ss[3]))
        ws = [jnp.exp(s_b - top) for s_b in ss]
        total = ws[0] + ws[1] + ws[2] + ws[3]
        acc = jnp.zeros((ROWS, WIDTH), F32)
        for b in range(4):
            v_b = fresh_ref[b].astype(F32)[r : r + 1, WIDTH:]
            acc = acc + ws[b].astype(BF16).astype(F32) * v_b
        tail[r] = acc / total
        tail_lse[r] = jnp.broadcast_to(top + jnp.log(total), (ROWS, WIDTH))

    arrive(*ARRIVE[1])

    for s in range(SLOTS):
        kv_copies[s].wait()
        kt[s] = kv[s, :, :WIDTH].T

    arrive(*(o for o in ARRIVE[2] if BELOW[o]))
    for i, dx in enumerate(X_PEERS):
        along_x[i].wait_recv()
        table_to_sibling(i, ((x - dx + NX) % NX) * NC + c)
    arrive(*(o for o in ARRIVE[2] if not BELOW[o]))
    arrive(*(o for o in ARRIVE[3] if BELOW[o]))

    for t in across:
        t.wait_recv()
    lane = lax.broadcasted_iota(jnp.int32, (1, WIDTH), 1)
    want = (((x * NZ + (lane % 32) // 2) * NC + c) * 2 + lane % 2) * 4 + lane // 32
    index = jnp.zeros((1, WIDTH), jnp.int32)
    for gg in range(GROUPS):
        for s in range(SLOTS):
            index = jnp.where(rowtab[gg, s] == want, gg * SLOTS + s, index)
    ivec[...] = index
    to_smem = [
        pltpu.make_async_copy(rowtab, tab_s, sm_sem.at[0]),
        pltpu.make_async_copy(ivec, ivec_s, sm_sem.at[1]),
    ]
    for copy in to_smem:
        copy.start()
    for copy in to_smem:
        copy.wait()

    arrive(*(o for o in ARRIVE[3] if not BELOW[o]), *ARRIVE[4])
    for t in hand:
        t.wait_recv()

    group = lax.broadcasted_iota(jnp.int32, (16, WIDTH), 0) // 4
    got = (got0, got1)

    def choose(gg, half, ref):
        lens = jnp.zeros((16, WIDTH), F32)
        for i in range(2):
            owner = tab_s[gg, 2 * half + i, 0, 0] // 4
            zz, cc, r = (owner // 4) % NZ, (owner // 2) % NC, owner % 2
            ref[4 * i : 4 * i + 4] = qall[zz, cc, pl.ds(4 * r, 4)]
            lens = jnp.where(group == i, qall[zz, cc, 8].astype(F32), lens)
        ref[8] = lens.astype(BF16)

    queries = []
    for half in range(2):
        for i, dx in enumerate(X_PEERS):
            choose(((x + dx) % NX) * NC + c, half, sel.at[i, half])
            copy = send(
                sel.at[i, half], got[half].at[x], s_ss.at[i, half], s_rs.at[i, half], at(dx, 0, 0, 0)
            )
            copy.start()
            queries.append(copy)
        choose(g, half, got[half].at[x])

    lane_pos = lax.broadcasted_iota(jnp.int32, (1, BLOCK), 1).astype(F32)
    lane_id = lax.broadcasted_iota(jnp.int32, (ROWS, WIDTH), 1)
    lcols = jnp.zeros((ROWS, WIDTH), F32)
    back, lse_sent = [], []
    for half in range(2):
        for t in queries[half * len(X_PEERS) : (half + 1) * len(X_PEERS)]:
            t.wait_recv()
        rounded, totals = [], []
        for n in range(2):
            s = 2 * half + n
            code = tab_s[g, s, 0, 0]
            owner, blk = code // 4, code % 4
            src = owner // 64
            r = owner % 2
            q = got[half][src, 4 * n : 4 * n + 4].reshape(ROWS, WIDTH)
            lens = got[half][src, 8].astype(F32)
            hi = jnp.where(r == 0, lens[4 * n : 4 * n + 1], lens[4 * n + 2 : 4 * n + 3])
            lo = jnp.where(r == 0, lens[4 * n + 1 : 4 * n + 2], lens[4 * n + 3 : 4 * n + 4])
            left = (hi * 64.0 + lo)[:, :1] - (blk * BLOCK).astype(F32)
            scores = jnp.dot(q, kt[s], preferred_element_type=F32)
            scores = jnp.where(lane_pos < left, scores, -jnp.inf)
            top = jnp.max(scores, axis=1, keepdims=True)
            weights = jnp.exp2((scores - top) * (SCALE * LOG2E))
            total = jnp.sum(weights, axis=1, keepdims=True)
            lcols = jnp.where(lane_id == s, top * SCALE + jnp.log(total), lcols)
            rounded.append(weights.astype(BF16))
            totals.append(total)
        if half == 1:
            lt = jnp.concatenate([lcols, lcols], axis=0).T
            for s in range(SLOTS):
                lses[g, s] = lt[s : s + 1]
            for i, to in enumerate(row):
                copy = send(lses.at[g], lses.at[g], l_ss.at[i], l_rs.at[i], to)
                copy.start()
                lse_sent.append(copy)
        for n in range(2):
            s = 2 * half + n
            part = jnp.dot(rounded[n], kv[s, :, WIDTH:], preferred_element_type=F32) / totals[n]
            parts[g, s] = part.astype(BF16).reshape(4, 16, WIDTH)
            if half == 0 and n == 0:
                continue
            mine = parts.at[g, s] if half else parts.at[g, 0:2]
            for i, to in enumerate(row if half else row[:4]):
                copy = send(mine, mine, p_ss.at[i, half * (n + 1)], p_rs.at[i, half * (n + 1)], to)
                copy.start()
                back.append(copy)
    for copy in [*spread.values(), *hand, *tables, *along_x, *across, *queries]:
        copy.wait_send()

    handed = []
    for i, dx in enumerate(X_PEERS):
        back[i].wait_recv()
        there = parts.at[((x - dx + NX) % NX) * NC + c, 0:2]
        copy = send(there, there, u_ss.at[i], u_rs.at[i], at(0, 0, 1, 0))
        copy.start()
        handed.append(copy)
    for copy in lse_sent:
        copy.wait_recv()

    wmat[...] = jnp.zeros((WIDTH, WIDTH), F32)
    away = lax.broadcasted_iota(jnp.int32, (NZ, WIDTH), 0)
    half = lax.broadcasted_iota(jnp.int32, (NZ, WIDTH), 1) // ROWS
    target = (((x * NZ + (z + away) % NZ) * NC + c) * 2 + half) * 4
    ls = [jnp.full((NZ, WIDTH), NEG, F32) for _ in range(3)]
    for gg in range(GROUPS):
        for s in range(SLOTS):
            here = rowtab[gg, s] - target
            lse = lses[gg, s]
            ls = [jnp.where(here == k, lse, ls[k]) for k in range(3)]
    peak = jnp.maximum(jnp.maximum(ls[0], ls[1]), ls[2])
    ws = [jnp.exp(l - peak) for l in ls]
    total = ws[0] + ws[1] + ws[2]
    merged = peak + jnp.log(total)
    for k in range(3):
        wmat[16 * k : 16 * (k + 1)] = ws[k] / total
    for d in range(NZ):
        clse[d] = merged[d : d + 1]
    wcol[...] = wmat[...].T

    def build(d):
        d = d % NZ
        for r in range(2):
            acc = jnp.zeros((ROWS, WIDTH), F32)
            for k in range(3):
                i = ivec_s[0, k * 32 + ((z + d) % NZ) * 2 + r]
                p = parts[i // 4, i % 4].reshape(ROWS, WIDTH).astype(F32)
                acc = acc + wcol[r * ROWS : (r + 1) * ROWS, k * 16 + d : k * 16 + d + 1] * p
            cbuf[d, 4 * r : 4 * r + 4] = acc.astype(BF16).reshape(4, 16, WIDTH)

    for copy in back[3:] + handed:
        copy.wait_recv()

    up = {}

    def start_up(o, data, lse):
        i = PLACE[o]
        to = at(0, PARENT[o] - o, 0, 0)
        up[o] = (
            send(lse, rlse.at[i], d_ss.at[i], d_rs.at[i], to),
            send(data, rbuf.at[i], c_ss.at[i], c_rs.at[i], to),
        )

    now = [o for o in LEAVES if PARENT[o] != 0]
    later = [o for o in LEAVES if o not in now]
    for o in now:
        build(-o)
        start_up(o, cbuf.at[-o % NZ], clse.at[-o % NZ])
        for copy in up[o]:
            copy.start()
    for o in (*HUBS, 0, *later):
        build(-o)
    for copy in [*back, *lse_sent, *handed]:
        copy.wait_send()

    def merge(hubs):
        columns = {}
        for o in hubs:
            for k in CHILDREN[o]:
                up[k][0].wait_recv()
            ls = [clse[-o % NZ]] + [rlse[PLACE[k]] for k in CHILDREN[o]]
            peak = ls[0]
            for l in ls[1:]:
                peak = jnp.maximum(peak, l)
            ws = [jnp.exp(l - peak) for l in ls]
            total = ws[0]
            for w in ws[1:]:
                total = total + w
            n = HUBS.index(o)
            mlse[n] = peak + jnp.log(total)
            start_up(o, mbuf.at[n], mlse.at[n])
            up[o][0].start()
            for i, w in enumerate(ws):
                wmat[i : i + 1] = w / total
            columns[o] = wmat[0:8].T
        for o in hubs:
            for k in CHILDREN[o]:
                up[k][1].wait_recv()
            data = [cbuf[-o % NZ]] + [rbuf[PLACE[k]] for k in CHILDREN[o]]
            acc = jnp.zeros((WIDTH, WIDTH), F32)
            for i, p in enumerate(data):
                acc = acc + columns[o][:, i : i + 1] * p.reshape(WIDTH, WIDTH).astype(F32)
            mbuf[HUBS.index(o)] = acc.astype(BF16).reshape(8, 16, WIDTH)
            up[o][1].start()

    for n in sorted({height(PARENT, o) for o in HUBS}):
        merge([o for o in HUBS if height(PARENT, o) == n])
        if n == 1:
            for o in later:
                start_up(o, cbuf.at[-o % NZ], clse.at[-o % NZ])
                for copy in up[o]:
                    copy.start()
    for o in up:
        if PARENT[o] != 0:
            for copy in up[o]:
                copy.wait_send()

    for k in CHILDREN[0]:
        up[k][0].wait_recv()
    for i, k in enumerate(CHILDREN[0]):
        wmat[i : i + 1] = rlse[PLACE[k]]
    wmat[len(CHILDREN[0]) : len(CHILDREN[0]) + 1] = clse[0]
    wt = wmat[0:8].T
    ends = []
    for r in range(2):
        rs = slice(r * ROWS, (r + 1) * ROWS)
        tl = tail_lse[r][:, :1]
        ls = [wt[rs, n : n + 1] for n in range(len(CHILDREN[0]) + 1)]
        peak = tl
        for l in ls:
            peak = jnp.maximum(peak, l)
        w = jnp.exp(tl - peak)
        ws = [jnp.exp(l - peak) for l in ls]
        denom = w
        for v in ws:
            denom = denom + v
        p = cbuf[0, 4 * r : 4 * r + 4].reshape(ROWS, WIDTH).astype(F32)
        ends.append((ws, denom, w * tail[r] + ws[-1] * p))
    for k in CHILDREN[0]:
        up[k][1].wait_recv()
    done = []
    for r in range(2):
        ws, denom, acc = ends[r]
        for n, k in enumerate(CHILDREN[0]):
            acc = acc + ws[n] * rbuf[PLACE[k], 4 * r : 4 * r + 4].reshape(ROWS, WIDTH).astype(F32)
        done.append(acc / denom)
    for a in range(4):
        heads = [
            jnp.concatenate([done[0][i : i + 1], done[1][i : i + 1]], axis=0)
            for i in range(16 * a, 16 * a + 16)
        ]
        out_ref[a] = jnp.concatenate(heads, axis=1).astype(BF16)

    for o in CHILDREN[0]:
        for copy in up[o]:
            copy.wait_send()


def shards(query, fresh_key_value, kv_pool, lengths, slot_owner, slot_block):
    dma = pltpu.SemaphoreType.DMA
    hbm = pl.BlockSpec(memory_space=pl.ANY)
    m = len(PARENT)
    return pl.pallas_call(
        kernel,
        out_shape=jax.ShapeDtypeStruct(query.shape, BF16),
        in_specs=[hbm] * 6,
        out_specs=pl.BlockSpec(memory_space=pltpu.VMEM),
        scratch_shapes=[
            pltpu.VMEM(query.shape, BF16),
            pltpu.VMEM((8, 16, WIDTH), BF16),
            pltpu.VMEM(fresh_key_value.shape, BF16),
            pltpu.SMEM(lengths.shape, jnp.int32),
            pltpu.SMEM(slot_owner.shape, jnp.int32),
            pltpu.SMEM(slot_block.shape, jnp.int32),
            pltpu.VMEM((SLOTS, BLOCK, 2 * WIDTH), BF16),
            pltpu.VMEM((SLOTS, WIDTH, BLOCK), BF16),
            pltpu.VMEM((NZ, NC, 9, 16, WIDTH), BF16),
            pltpu.VMEM((GROUPS, SLOTS, 1, WIDTH), jnp.int32),
            pltpu.VMEM((1, WIDTH), jnp.int32),
            pltpu.SMEM((GROUPS, SLOTS, 1, WIDTH), jnp.int32),
            pltpu.SMEM((1, WIDTH), jnp.int32),
            pltpu.VMEM((3, 2, 9, 16, WIDTH), BF16),
            pltpu.VMEM((NX, 9, 16, WIDTH), BF16),
            pltpu.VMEM((NX, 9, 16, WIDTH), BF16),
            pltpu.VMEM((GROUPS, SLOTS, 4, 16, WIDTH), BF16),
            pltpu.VMEM((GROUPS, SLOTS, 1, WIDTH), F32),
            pltpu.VMEM((WIDTH, WIDTH), F32),
            pltpu.VMEM((WIDTH, WIDTH), F32),
            pltpu.VMEM((NZ, 8, 16, WIDTH), BF16),
            pltpu.VMEM((NZ, 1, WIDTH), F32),
            pltpu.VMEM((m, 8, 16, WIDTH), BF16),
            pltpu.VMEM((m, 1, WIDTH), F32),
            pltpu.VMEM((len(HUBS), 8, 16, WIDTH), BF16),
            pltpu.VMEM((len(HUBS), 1, WIDTH), F32),
            pltpu.VMEM((2, ROWS, WIDTH), F32),
            pltpu.VMEM((2, ROWS, WIDTH), F32),
            dma((5,)),
            dma((SLOTS,)),
            dma((2,)),
            dma((3,)), dma((3,)),
            dma((3,)), dma((3,)),
            dma((4,)), dma((4,)),
            dma((m,)), dma((m,)),
            dma((m + 1,)), dma((m + 1,)),
            dma((3, 2)), dma((3, 2)),
            dma((7, 3)), dma((7, 3)),
            dma((7,)), dma((7,)),
            dma((3,)), dma((3,)),
            dma((m,)), dma((m,)),
            dma((m,)), dma((m,)),
        ],
        compiler_params=pltpu.CompilerParams(
            collective_id=0, has_side_effects=True, vmem_limit_bytes=60 << 20
        ),
        name="lent_attention",
    )(query, fresh_key_value, kv_pool, lengths, slot_owner, slot_block)


def solution(mesh):
    placed = (
        P(None, "inst", "tp"),
        P(None, "inst", "tp"),
        P("inst", None, "tp"),
        P("inst"),
        P(("inst", "tp")),
        P(("inst", "tp")),
    )
    return jax.shard_map(
        shards, mesh=mesh, in_specs=placed, out_specs=P(None, "inst", "tp"), check_vma=False
    )
```
